256 devices in a mesh: bump: 4 (over y), nx: 16 (over x_lo, z), ny: 4 (over x_hi, core).
Axes of the slice: x: 4 (x_hi: 2, x_lo: 2; x = x_hi * 2 + x_lo), y: 4, z: 8, core: 2. Of those that a mesh axis runs over, the one named last changes fastest.
Arguments:
- payoff: float32 [2097152], P(('nx', 'ny')), may hold values from -6 to 6
- positions: float32 [2097152], P(('nx', 'ny')), may hold values from -20 to 20
- tables: float32 [8, 5, 2097152], P('bump', None, ('nx', 'ny')), may hold values from 0.02 to 1, as said below
- offsets: int32 [8, 8192], P(None, ('nx', 'ny')), may hold values from -1 to 1
- vol_curve: float32 [8], replicated, may hold values from 0.5 to 1.2
- bucket: int32 [64], P('bump'), may hold values from 0 to 7
- bump_size: float32 [64], P('bump'), may hold values from 0.1 to 0.4
Outputs:
- bumped_values: float32 [64, 2097152], P('bump', ('nx', 'ny'))
- vega: float32 [64], P('bump')
The draws below stay inside these ranges and needn't reach their ends.
Inputs may be any that keep to these rules, and one draw needn't show every extreme that they name: `tables`: component 0 lies in [0.9, 1], components 1 and 3 in [0.1, 0.2], components 2 and 4 in [0.02, 0.06].
All inputs are finite; a program needn't handle non-finite values.
Results may differ from the reference program's by a relative error of at most 0.0003.
Values sent between devices are 32-bit elements; how exact they have to be, the bound alone decides.
No kernel may reach another device: no remote copies, remote signals or barrier semaphores. Data moves between devices by JAX's collectives and lax.ppermute only.
A program may use at most 64 MiB of HBM per device.

```python
import math
import jax
import jax.numpy as jnp
from jax import lax

STEPS = 8
BLOCK = 256
NODES = 2097152
BUMPS = 64


def draw_tables(key, part):
    lower = jnp.array([0.9, 0.1, 0.02, 0.1, 0.02], jnp.float32)
    upper = jnp.array([1.0, 0.2, 0.06, 0.2, 0.06], jnp.float32)
    unit = jax.random.uniform(key, (STEPS, 5, NODES), jnp.float32)
    return lower[None, :, None] + (upper - lower)[None, :, None] * unit


def draw_positions(key, part):
    ramp = jnp.exp(jnp.log(3.0) * jnp.arange(NODES, dtype=jnp.float32) / NODES)
    noise = jax.random.normal(key, (NODES,), jnp.float32)
    return jnp.clip(noise * ramp, -6.0, 6.0) * 2.0


def set_ends(values, own_key, least, largest):
    place = [jax.random.randint(jax.random.fold_in(own_key, axis), (), 0, length) for axis, length in enumerate(values.shape)]
    main_axis = values.shape.index(max(values.shape))
    next_to = place[:main_axis] + [(place[main_axis] + 1) % values.shape[main_axis]] + place[main_axis + 1:]
    return values.at[tuple(place)].set(least).at[tuple(next_to)].set(largest)


def block_levels(rng, shape, cuts, least, top_value):
    loudness, own = 1.0, jax.random.fold_in(rng, 6)
    for axis_at, parts in cuts:
        steps = jnp.exp(jax.random.uniform(jax.random.fold_in(own, axis_at), (parts,), jnp.float32, least / len(cuts), top_value / len(cuts)))
        loudness = loudness * jnp.repeat(steps, shape[axis_at] // parts).reshape([-1 if axis == axis_at else 1 for axis in range(len(shape))])
    return loudness


def gaussian(rng, dims, deviation, most, pieces=(), kind=jnp.bfloat16):
    gain = block_levels(rng, dims, pieces, -0.22, 0.18) if pieces else 1.0
    values = jax.random.normal(rng, dims, jnp.float32) * deviation * gain
    return jnp.minimum(jnp.maximum(values, -most), most).astype(kind)


def setup_inputs(seed: int = 0) -> dict:
    key_of = jax.random.split(jax.random.key(seed), 8)
    payoff = gaussian(key_of[0], (NODES,), 1.0, 6.0, ((0, 64),), jnp.float32)
    positions = draw_positions(jax.random.fold_in(key_of[7], 71), 0)
    tables = draw_tables(jax.random.fold_in(key_of[7], 71), 0)
    offsets = set_ends(jax.random.randint(key_of[3], (STEPS, NODES // BLOCK), -1, 2), jax.random.fold_in(key_of[3], 1), -1, 1).astype(jnp.int32)
    vol_curve = jnp.clip(jnp.exp(jax.random.uniform(key_of[4], (STEPS,), jnp.float32, math.log(0.5), math.log(1.2))), 0.5, 1.2)
    bucket = set_ends(jax.random.randint(key_of[5], (BUMPS,), 0, STEPS), jax.random.fold_in(key_of[5], 1), 0, STEPS - 1).astype(jnp.int32)
    bump_size = jnp.clip(jnp.exp(math.log(0.4) - 1.3862944 * jax.random.uniform(key_of[6], (BUMPS,), jnp.float32) ** block_levels(key_of[6], (BUMPS,), ((0, 4),), -0.2, 0.2)), 0.1, 0.4)
    return dict(payoff=payoff, positions=positions, tables=tables, offsets=offsets, vol_curve=vol_curve, bucket=bucket, bump_size=bump_size)


def advance(padded, table, branch_nodes, variance):
    count = padded.shape[-1] - 4

    def shifted(shift_by):
        return padded[..., 2 + shift_by:2 + shift_by + count]

    upward = table[1] + variance * table[2]
    downward = table[3] + variance * table[4]
    middle = 1.0 - upward - downward
    low_case = upward * shifted(0) + middle * shifted(-1) + downward * shifted(-2)
    even_case = upward * shifted(1) + middle * shifted(0) + downward * shifted(-1)
    high_case = upward * shifted(2) + middle * shifted(1) + downward * shifted(0)
    mixed = jnp.where(branch_nodes == -1, low_case, jnp.where(branch_nodes == 0, even_case, high_case))
    return table[0] * mixed


def reference(payoff, positions, tables, offsets, vol_curve, bucket, bump_size):
    block_len = NODES // offsets.shape[1]

    def rollback(variance_row):
        values = payoff
        for step in reversed(range(STEPS)):
            padded = jnp.pad(values, 2, mode="wrap")
            branch_nodes = jnp.repeat(offsets[step], block_len)
            values = advance(padded, tables[step], branch_nodes, variance_row[step])
        return values

    base_values = rollback(vol_curve * vol_curve)
    step_ids = jnp.arange(STEPS, dtype=jnp.int32)
    sigma_rows = vol_curve[None, :] + bump_size[:, None] * (bucket[:, None] == step_ids[None, :]).astype(jnp.float32)

    def one_curve(variance_row):
        values = rollback(variance_row)
        return values, jnp.sum(positions * (values - base_values))

    bumped_values, weighted = lax.map(one_curve, sigma_rows * sigma_rows)
    return bumped_values, weighted / bump_size
```

```python
import jax
import jax.numpy as jnp
from jax import lax
from jax.experimental import pallas as pl
from jax.experimental.pallas import tpu as pltpu
from jax.sharding import PartitionSpec as P

NODE_AXES = ("nx", "ny")
LANES = 128
ROWS_PER_STEP = 5
STEPS = 8
WORKERS = 4
LOCAL_STEPS = STEPS // WORKERS
LOCAL_ROWS = LOCAL_STEPS * ROWS_PER_STEP
CURVES = 16
VMEM_LIMIT = 48 * 1024 * 1024

ROWS = 256
CHUNK = ROWS // WORKERS
PADDED = CHUNK + 8
PAIRS = LOCAL_STEPS * ROWS
CHUNK_PAIRS = LOCAL_STEPS * CHUNK
PADDED_PAIRS = LOCAL_STEPS * PADDED
TABLE_ROWS = LOCAL_ROWS * CHUNK
GHOST_ROWS = 24
MESSAGE = TABLE_ROWS + GHOST_ROWS
HALO = 24
VALUES = (STEPS + 1) * CHUNK

EXPAND_COST = pl.CostEstimate(flops=100_000_000, bytes_accessed=100_000_000, transcendentals=0)

VMEM = pltpu.MemorySpace.VMEM
SMEM = pltpu.MemorySpace.SMEM


def params(limit=VMEM_LIMIT):
    return pltpu.CompilerParams(vmem_limit_bytes=limit)


def vmem():
    return pl.BlockSpec(memory_space=VMEM)


def smem():
    return pl.BlockSpec(memory_space=SMEM)


def anywhere():
    return pl.BlockSpec(memory_space=pl.ANY)


def in_hbm(array):
    return pltpu.with_memory_space_constraint(array, pltpu.HBM)


def hbm():
    return pl.BlockSpec(memory_space=pltpu.HBM)


def edges_kernel(tables, payoff, offsets, first, last, held, held_payoff, held_offsets, sem):
    copies = [pltpu.make_async_copy(offsets, held_offsets, sem.at[2, 0])]
    for side, pair, row in ((0, 0, 0), (1, PAIRS - 8, ROWS - 8)):
        copies.append(
            pltpu.make_async_copy(tables.at[:, pl.ds(pair, 8), :], held.at[side], sem.at[0, side])
        )
        copies.append(
            pltpu.make_async_copy(
                payoff.at[pl.ds(row, 8), :], held_payoff.at[side], sem.at[1, side]
            )
        )
    for copy in copies:
        copy.start()
    for copy in copies:
        copy.wait()
    for side, out, row, lane in ((0, first, 0, 0), (1, last, 7, LANES - 1)):
        pair = row * (8 - LOCAL_STEPS) // 7
        for i in range(ROWS_PER_STEP):
            out[i * LOCAL_STEPS : (i + 1) * LOCAL_STEPS, :] = held[
                side, i, pair : pair + LOCAL_STEPS, :
            ]
        out[LOCAL_ROWS : 2 * STEPS, :] = jnp.broadcast_to(
            held_payoff[side, row : row + 1, :], (2 * STEPS - LOCAL_ROWS, LANES)
        )
        out[2 * STEPS : HALO, :] = jnp.broadcast_to(
            held_offsets[:, lane : lane + 1].astype(jnp.float32), (STEPS, LANES)
        )


def edges(tables, payoff_rows, offsets):
    shape = jax.ShapeDtypeStruct((HALO, LANES), jnp.float32)
    return pl.pallas_call(
        edges_kernel,
        out_shape=(shape, shape),
        in_specs=[hbm(), hbm(), hbm()],
        out_specs=(vmem(), vmem()),
        scratch_shapes=[
            pltpu.VMEM((2, ROWS_PER_STEP, 8, LANES), jnp.float32),
            pltpu.VMEM((2, 8, LANES), jnp.float32),
            pltpu.VMEM((STEPS, LANES), jnp.int32),
            pltpu.SemaphoreType.DMA((3, 2)),
        ],
        compiler_params=params(),
        name="edges",
    )(*(in_hbm(array) for array in (tables, payoff_rows, offsets)))


def load_kernel(tables, payoff, positions, held, held_payoff, held_positions, sem):
    copies = [
        pltpu.make_async_copy(source, target, sem.at[i])
        for i, (source, target) in enumerate(
            ((tables, held), (payoff, held_payoff), (positions, held_positions))
        )
    ]
    for copy in copies:
        copy.start()
    for copy in copies:
        copy.wait()


def load(*arrays):
    return pl.pallas_call(
        load_kernel,
        out_shape=tuple(jax.ShapeDtypeStruct(array.shape, array.dtype) for array in arrays),
        in_specs=[hbm()] * len(arrays),
        out_specs=(vmem(),) * len(arrays),
        scratch_shapes=[pltpu.SemaphoreType.DMA((len(arrays),))],
        compiler_params=params(),
        cost_estimate=pl.CostEstimate(flops=0, bytes_accessed=6_000_000, transcendentals=0),
        name="load",
    )(*(in_hbm(array) for array in arrays))


def pack_kernel(tables, before, after, own, plus1, plus2, plus3):
    me = lax.axis_index("bump")
    for k, out in ((1, plus1), (3, plus3), (2, plus2), (0, own)):
        chunk = lax.rem(me + k, WORKERS)
        below = lax.rem(chunk + WORKERS - 1, WORKERS)
        above = lax.rem(chunk + 1, WORKERS)
        start = pl.multiple_of(chunk * CHUNK_PAIRS, CHUNK_PAIRS)
        low = pl.multiple_of(below * CHUNK_PAIRS + CHUNK_PAIRS - 8, 8)
        high = pl.multiple_of(above * CHUNK_PAIRS, CHUNK_PAIRS)
        for i in range(ROWS_PER_STEP):
            out[i * CHUNK_PAIRS : (i + 1) * CHUNK_PAIRS, :] = tables[i, pl.ds(start, CHUNK_PAIRS), :]
            two = slice(i * LOCAL_STEPS, (i + 1) * LOCAL_STEPS)
            row = TABLE_ROWS + i * LOCAL_STEPS
            out[row : row + LOCAL_STEPS, :] = jnp.where(
                chunk == 0, before[two, :], tables[i, pl.ds(low, 8), :][8 - LOCAL_STEPS :]
            )
            row += LOCAL_ROWS
            out[row : row + LOCAL_STEPS, :] = jnp.where(
                chunk == WORKERS - 1, after[two, :], tables[i, pl.ds(high, 8), :][:LOCAL_STEPS]
            )
        out[TABLE_ROWS + 2 * LOCAL_ROWS :, :] = jnp.zeros(
            (GHOST_ROWS - 2 * LOCAL_ROWS, LANES), jnp.float32
        )


def pack(tables, before, after):
    shape = jax.ShapeDtypeStruct((MESSAGE, LANES), jnp.float32)
    return pl.pallas_call(
        pack_kernel,
        out_shape=(shape,) * WORKERS,
        in_specs=[vmem()] * 3,
        out_specs=(vmem(),) * WORKERS,
        compiler_params=params(),
        name="pack",
    )(tables, before, after)


def shifted(values, by, lane):
    if by == 0:
        return values
    turned = pltpu.roll(values, (-by) % LANES, 1)
    if by > 0:
        return jnp.where(lane < LANES - by, turned, pltpu.roll(turned, PADDED - 1, 0))
    return jnp.where(lane >= -by, turned, pltpu.roll(turned, 1, 0))


def spread(low, even, down, middle, up):
    zero = jnp.zeros_like(up)
    return (
        jnp.where(low, down, zero),
        jnp.where(low, middle, jnp.where(even, down, zero)),
        jnp.where(low, up, jnp.where(even, middle, down)),
        jnp.where(low, zero, jnp.where(even, up, middle)),
        jnp.where(even, zero, up),
    )


def weigh(weights, reach):
    total = weights[0] * reach[0]
    for weight, value in zip(weights[1:], reach[1:]):
        total = total + weight * value
    return total


def roll_kernel(
    own,
    from_m1,
    from_m2,
    from_p1,
    payoff,
    positions,
    offsets,
    before,
    after,
    vol,
    out,
    sums,
    table,
    steps_k,
    nodes_k,
):
    me = lax.axis_index("bump")
    sources = (own, from_m1, from_m2, from_p1)
    turns = (0, WORKERS - 1, WORKERS - 2, 1)
    turned = jnp.transpose(offsets[...].astype(jnp.float32))
    steps_k[8 : 8 + ROWS, :] = jnp.repeat(turned, ROWS // LANES, axis=0)
    steps_k[0:8, :] = jnp.transpose(before[2 * STEPS : HALO, 0:8])
    steps_k[8 + ROWS :, :] = jnp.transpose(after[2 * STEPS : HALO, 0:8])
    start = pl.multiple_of(me * CHUNK, CHUNK)
    part = jnp.concatenate(
        [
            steps_k[pl.ds(start + 8, CHUNK + 1), :],
            jnp.zeros((PADDED - CHUNK - 2, STEPS), jnp.float32),
            steps_k[pl.ds(start + 7, 1), :],
        ]
    )
    for s in range(STEPS):
        nodes_k[s] = jnp.broadcast_to(part[:, s : s + 1], (PADDED, LANES))
    above = payoff[pl.ds(pl.multiple_of(jnp.minimum(start + CHUNK, ROWS - 8), 8), 8), :]
    below = payoff[pl.ds(pl.multiple_of(jnp.maximum(start - 8, 0), 8), 8), :]
    values = jnp.concatenate(
        [
            payoff[pl.ds(start, CHUNK), :],
            jnp.where(me == WORKERS - 1, after[LOCAL_ROWS : LOCAL_ROWS + 1, :], above[0:1, :]),
            jnp.zeros((PADDED - CHUNK - 2, LANES), jnp.float32),
            jnp.where(me == 0, before[LOCAL_ROWS : LOCAL_ROWS + 1, :], below[7:8, :]),
        ]
    )
    gap = jnp.zeros((PADDED_PAIRS - CHUNK_PAIRS - 2 * LOCAL_STEPS, LANES), jnp.float32)
    for k in range(WORKERS):
        owner = lax.rem(me + turns[k], WORKERS)
        source = sources[k]
        for i in range(ROWS_PER_STEP):
            table[owner, i, :CHUNK_PAIRS, :] = source[i * CHUNK_PAIRS : (i + 1) * CHUNK_PAIRS, :]
            low = TABLE_ROWS + i * LOCAL_STEPS
            high = low + LOCAL_ROWS
            table[owner, i, CHUNK_PAIRS:, :] = jnp.concatenate(
                [source[high : high + LOCAL_STEPS, :], gap, source[low : low + LOCAL_STEPS, :]]
            )

    def rows(s, i):
        return table[s // LOCAL_STEPS, i, pl.ds(s % LOCAL_STEPS, PADDED, stride=LOCAL_STEPS), :]

    lane = lax.broadcasted_iota(jnp.int32, (PADDED, LANES), 1)
    slopes = {}
    for s in reversed(range(STEPS)):
        variance = vol[s] * vol[s]
        discount = rows(s, 0)
        up_slope = discount * rows(s, 2)
        down_slope = discount * rows(s, 4)
        up = discount * rows(s, 1) + variance * up_slope
        down = discount * rows(s, 3) + variance * down_slope
        low, even = nodes_k[s] < -0.5, nodes_k[s] < 0.5
        weights = spread(low, even, down, discount - up - down, up)
        slope_weights = spread(low, even, down_slope, -(up_slope + down_slope), up_slope)
        for q in list(slopes):
            reach = [shifted(slopes[q], m, lane) for m in range(-2, 3)]
            slopes[q] = weigh(weights, reach)
        reach = [shifted(values, m, lane) for m in range(-2, 3)]
        slopes[s] = weigh(slope_weights, reach)
        values = weigh(weights, reach)
    out[0:CHUNK, :] = values[0:CHUNK]
    weight = positions[pl.ds(start, CHUNK), :]
    for s in range(STEPS):
        slope = slopes[s][0:CHUNK]
        out[(s + 1) * CHUNK : (s + 2) * CHUNK, :] = slope
        sums[s : s + 1, :] = jnp.sum(weight * slope, axis=0, keepdims=True)


def share_kernel(own, from_m1, from_m2, from_p1, out):
    added = own[...] + from_m1[...] + from_m2[...] + from_p1[...]
    totals = jnp.sum(added, axis=1, keepdims=True)
    lane = lax.broadcasted_iota(jnp.int32, (STEPS, LANES), 1)
    step = lax.broadcasted_iota(jnp.int32, (STEPS, LANES), 0)
    row = jnp.sum(jnp.where(lane == step, totals, 0.0), axis=0, keepdims=True)
    out[...] = jnp.broadcast_to(row, out.shape)


def share(parts, peers):
    return pl.pallas_call(
        share_kernel,
        out_shape=jax.ShapeDtypeStruct((peers, LANES), jnp.float32),
        in_specs=[vmem()] * WORKERS,
        out_specs=vmem(),
        compiler_params=params(),
        name="share",
    )(*parts)


def roll_back(messages, payoff, positions, offsets, before, after, vol):
    return pl.pallas_call(
        roll_kernel,
        out_shape=(
            jax.ShapeDtypeStruct((VALUES, LANES), jnp.float32),
            jax.ShapeDtypeStruct((STEPS, LANES), jnp.float32),
        ),
        in_specs=[vmem()] * (WORKERS + 5) + [smem()],
        out_specs=(vmem(), vmem()),
        scratch_shapes=[
            pltpu.VMEM((WORKERS, ROWS_PER_STEP, PADDED_PAIRS, LANES), jnp.float32),
            pltpu.VMEM((ROWS + 16, STEPS), jnp.float32),
            pltpu.VMEM((STEPS, PADDED, LANES), jnp.float32),
        ],
        compiler_params=params(),
        name="roll_back",
    )(*messages, payoff, positions, offsets, before, after, vol)


def expand_kernel(
    own, from_m1, from_m2, from_p1, vol, bucket, bump, out, rate, built, done
):
    me = lax.axis_index("bump")
    sources = (own, from_m1, from_m2, from_p1)
    turns = (0, WORKERS - 1, WORKERS - 2, 1)
    for b in range(CURVES):
        rate[b] = 2.0 * vol[bucket[b]] + bump[b]
    stores = []
    for k in range(WORKERS):
        chunk = lax.rem(me + turns[k], WORKERS)
        base = sources[k][0:CHUNK, :]
        for b in range(CURVES):
            gain = bump[b] * rate[b]
            at = pl.multiple_of((bucket[b] + 1) * CHUNK, CHUNK)
            slope = sources[k][pl.ds(at, CHUNK), :]
            built[b // 8, k, pl.ds(b % 8, CHUNK, stride=8), :] = base + gain * slope
        for tile in range(CURVES // 8):
            stores.append(
                pltpu.make_async_copy(
                    built.at[tile, k],
                    out.at[tile, pl.ds(pl.multiple_of(chunk * CHUNK * 8, CHUNK * 8), CHUNK * 8), :],
                    done.at[tile, k],
                )
            )
            stores[-1].start()
    for store in stores:
        store.wait()


def expand(parts, vol, bucket, bump):
    tiles = CURVES // 8
    laid, rate = pl.pallas_call(
        expand_kernel,
        out_shape=(
            jax.ShapeDtypeStruct((tiles, ROWS * 8, LANES), jnp.float32),
            jax.ShapeDtypeStruct((CURVES,), jnp.float32),
        ),
        in_specs=[vmem()] * WORKERS + [smem()] * 3,
        out_specs=(anywhere(), smem()),
        scratch_shapes=[
            pltpu.VMEM((tiles, WORKERS, CHUNK * 8, LANES), jnp.float32),
            pltpu.SemaphoreType.DMA((tiles, WORKERS)),
        ],
        compiler_params=params(),
        cost_estimate=EXPAND_COST,
        name="expand",
    )(*parts, vol, bucket, bump)
    curves = laid.reshape(tiles, ROWS, 8, LANES).transpose(0, 2, 1, 3)
    return curves.reshape(CURVES, ROWS * LANES), rate


def vega_kernel(shared, bucket, rate, vega):
    totals = jnp.sum(shared[...], axis=0, keepdims=True)
    lane = lax.broadcasted_iota(jnp.int32, (1, LANES), 1)
    for b in range(CURVES):
        vega[b] = rate[b] * jnp.sum(jnp.where(lane == bucket[b], totals, 0.0))


def vegas(shared, bucket, rate):
    return pl.pallas_call(
        vega_kernel,
        out_shape=jax.ShapeDtypeStruct((CURVES,), jnp.float32),
        in_specs=[vmem(), smem(), smem()],
        out_specs=smem(),
        compiler_params=params(),
        name="vegas",
    )(shared, bucket, rate)


def rotated(by):
    return [(i, (i + by) % WORKERS) for i in range(WORKERS)]


def exchanged(array, axis):
    return (array,) + tuple(lax.ppermute(array, axis, rotated(by)) for by in (1, 2, -1))


def on_device(payoff, positions, tables, offsets, vol_curve, bucket, bump_size):
    groups = lax.axis_size(NODE_AXES)
    up = [(i, (i + 1) % groups) for i in range(groups)]
    payoff_rows = payoff.reshape(ROWS, LANES)
    tables = tables.transpose(1, 0, 2).reshape(ROWS_PER_STEP, LOCAL_STEPS, ROWS, LANES)
    tables = tables.transpose(0, 2, 1, 3).reshape(ROWS_PER_STEP, PAIRS, LANES)
    first, last = edges(tables, payoff_rows, offsets)
    before = lax.ppermute(last, NODE_AXES, up)
    after = lax.ppermute(first, NODE_AXES, [(b, a) for a, b in up])
    held, payoff_rows, position_rows = load(tables, payoff_rows, positions.reshape(ROWS, LANES))
    messages = pack(held, before, after)
    received = (
        messages[0],
        lax.ppermute(messages[1], "bump", rotated(1)),
        lax.ppermute(messages[2], "bump", rotated(2)),
        lax.ppermute(messages[3], "bump", rotated(-1)),
    )
    arrays, sums = roll_back(
        received, payoff_rows, position_rows, offsets, before, after, vol_curve
    )
    inner, outer = "ny", ("bump", "nx")
    arrays, *sums = lax.optimization_barrier((arrays, *exchanged(sums, inner)))
    peers = lax.axis_size(outer)
    sums = share(sums, peers)
    bumped_values, rate = expand(exchanged(arrays, "bump"), vol_curve, bucket, bump_size)
    shared = lax.all_to_all(
        sums.reshape(peers, 1, LANES), outer, split_axis=0, concat_axis=0, tiled=True
    )
    return (bumped_values, vegas(shared.reshape(peers, LANES), bucket, rate))


def solution(mesh):
    in_specs = (
        P(("nx", "ny")),
        P(("nx", "ny")),
        P("bump", None, ("nx", "ny")),
        P(None, ("nx", "ny")),
        P(),
        P("bump"),
        P("bump"),
    )
    out_specs = (P("bump", ("nx", "ny")), P("bump"))
    return jax.shard_map(
        on_device, mesh=mesh, in_specs=in_specs, out_specs=out_specs, check_vma=False
    )
```

```python
import jax
import jax.numpy as jnp
from jax import lax
from jax.experimental import pallas as pl
from jax.experimental.pallas import tpu as pltpu
from jax.sharding import PartitionSpec as P

NODE_AXES = ("nx", "ny")
LANES = 128
ROWS_PER_STEP = 5
STEPS = 8
WORKERS = 4
LOCAL_STEPS = STEPS // WORKERS
LOCAL_ROWS = LOCAL_STEPS * ROWS_PER_STEP
CURVES = 16
VMEM_LIMIT = 48 * 1024 * 1024

ROWS = 256
CHUNK = ROWS // WORKERS
PADDED = CHUNK + 8
PAIRS = LOCAL_STEPS * ROWS
CHUNK_PAIRS = LOCAL_STEPS * CHUNK
PADDED_PAIRS = LOCAL_STEPS * PADDED
TABLE_ROWS = LOCAL_ROWS * CHUNK
GHOST_ROWS = 24
MESSAGE = TABLE_ROWS + GHOST_ROWS
HALO = 24
VALUES = (STEPS + 1) * CHUNK

EXPAND_COST = pl.CostEstimate(flops=100_000_000, bytes_accessed=100_000_000, transcendentals=0)

VMEM = pltpu.MemorySpace.VMEM
SMEM = pltpu.MemorySpace.SMEM


def params(limit=VMEM_LIMIT):
    return pltpu.CompilerParams(vmem_limit_bytes=limit)


def vmem():
    return pl.BlockSpec(memory_space=VMEM)


def smem():
    return pl.BlockSpec(memory_space=SMEM)


def anywhere():
    return pl.BlockSpec(memory_space=pl.ANY)


def in_hbm(array):
    return pltpu.with_memory_space_constraint(array, pltpu.HBM)


def hbm():
    return pl.BlockSpec(memory_space=pltpu.HBM)


def on_even_group():
    return lax.rem(lax.axis_index("ny"), 2) == 0


def halos(one, two):
    even = on_even_group()
    return jnp.where(even, two[...], one[...]), jnp.where(even, one[...], two[...])


def edges_kernel(tables, payoff, offsets, one, two, held, held_payoff, held_offsets, ends, sem):
    copies = [pltpu.make_async_copy(offsets, held_offsets, sem.at[2, 0])]
    for side, pair, row in ((0, 0, 0), (1, PAIRS - 8, ROWS - 8)):
        copies.append(
            pltpu.make_async_copy(tables.at[:, pl.ds(pair, 8), :], held.at[side], sem.at[0, side])
        )
        copies.append(
            pltpu.make_async_copy(
                payoff.at[pl.ds(row, 8), :], held_payoff.at[side], sem.at[1, side]
            )
        )
    for copy in copies:
        copy.start()
    for copy in copies:
        copy.wait()
    for side, row, lane in ((0, 0, 0), (1, 7, LANES - 1)):
        out = ends.at[side]
        pair = row * (8 - LOCAL_STEPS) // 7
        for i in range(ROWS_PER_STEP):
            out[i * LOCAL_STEPS : (i + 1) * LOCAL_STEPS, :] = held[
                side, i, pair : pair + LOCAL_STEPS, :
            ]
        out[LOCAL_ROWS : 2 * STEPS, :] = jnp.broadcast_to(
            held_payoff[side, row : row + 1, :], (2 * STEPS - LOCAL_ROWS, LANES)
        )
        out[2 * STEPS : HALO, :] = jnp.broadcast_to(
            held_offsets[:, lane : lane + 1].astype(jnp.float32), (STEPS, LANES)
        )
    one[...] = jnp.where(on_even_group(), ends[1], ends[0])
    two[...] = jnp.where(on_even_group(), ends[0], ends[1])


def edges(tables, payoff_rows, offsets):
    shape = jax.ShapeDtypeStruct((HALO, LANES), jnp.float32)
    return pl.pallas_call(
        edges_kernel,
        out_shape=(shape, shape),
        in_specs=[hbm(), hbm(), hbm()],
        out_specs=(vmem(), vmem()),
        scratch_shapes=[
            pltpu.VMEM((2, ROWS_PER_STEP, 8, LANES), jnp.float32),
            pltpu.VMEM((2, 8, LANES), jnp.float32),
            pltpu.VMEM((STEPS, LANES), jnp.int32),
            pltpu.VMEM((2, HALO, LANES), jnp.float32),
            pltpu.SemaphoreType.DMA((3, 2)),
        ],
        compiler_params=params(),
        name="edges",
    )(*(in_hbm(array) for array in (tables, payoff_rows, offsets)))


def load_kernel(tables, payoff, positions, held, held_payoff, held_positions, sem):
    copies = [
        pltpu.make_async_copy(source, target, sem.at[i])
        for i, (source, target) in enumerate(
            ((tables, held), (payoff, held_payoff), (positions, held_positions))
        )
    ]
    for copy in copies:
        copy.start()
    for copy in copies:
        copy.wait()


def load(*arrays):
    return pl.pallas_call(
        load_kernel,
        out_shape=tuple(jax.ShapeDtypeStruct(array.shape, array.dtype) for array in arrays),
        in_specs=[hbm()] * len(arrays),
        out_specs=(vmem(),) * len(arrays),
        scratch_shapes=[pltpu.SemaphoreType.DMA((len(arrays),))],
        compiler_params=params(),
        cost_estimate=pl.CostEstimate(flops=0, bytes_accessed=6_000_000, transcendentals=0),
        name="load",
    )(*(in_hbm(array) for array in arrays))


def pack_kernel(tables, one, two, own, plus1, plus2, plus3):
    me = lax.axis_index("bump")
    before, after = halos(one, two)
    for k, out in ((1, plus1), (3, plus3), (2, plus2), (0, own)):
        chunk = lax.rem(me + k, WORKERS)
        below = lax.rem(chunk + WORKERS - 1, WORKERS)
        above = lax.rem(chunk + 1, WORKERS)
        start = pl.multiple_of(chunk * CHUNK_PAIRS, CHUNK_PAIRS)
        low = pl.multiple_of(below * CHUNK_PAIRS + CHUNK_PAIRS - 8, 8)
        high = pl.multiple_of(above * CHUNK_PAIRS, CHUNK_PAIRS)
        for i in range(ROWS_PER_STEP):
            out[i * CHUNK_PAIRS : (i + 1) * CHUNK_PAIRS, :] = tables[i, pl.ds(start, CHUNK_PAIRS), :]
            at = slice(i * LOCAL_STEPS, (i + 1) * LOCAL_STEPS)
            row = TABLE_ROWS + i * LOCAL_STEPS
            out[row : row + LOCAL_STEPS, :] = jnp.where(
                chunk == 0, before[at, :], tables[i, pl.ds(low, 8), :][8 - LOCAL_STEPS :]
            )
            row += LOCAL_ROWS
            out[row : row + LOCAL_STEPS, :] = jnp.where(
                chunk == WORKERS - 1, after[at, :], tables[i, pl.ds(high, 8), :][:LOCAL_STEPS]
            )
        out[TABLE_ROWS + 2 * LOCAL_ROWS :, :] = jnp.zeros(
            (GHOST_ROWS - 2 * LOCAL_ROWS, LANES), jnp.float32
        )


def pack(tables, one, two):
    shape = jax.ShapeDtypeStruct((MESSAGE, LANES), jnp.float32)
    return pl.pallas_call(
        pack_kernel,
        out_shape=(shape,) * WORKERS,
        in_specs=[vmem()] * 3,
        out_specs=(vmem(),) * WORKERS,
        compiler_params=params(),
        name="pack",
    )(tables, one, two)


def shifted(values, by, lane):
    if by == 0:
        return values
    turned = pltpu.roll(values, (-by) % LANES, 1)
    if by > 0:
        return jnp.where(lane < LANES - by, turned, pltpu.roll(turned, PADDED - 1, 0))
    return jnp.where(lane >= -by, turned, pltpu.roll(turned, 1, 0))


def spread(low, even, down, middle, up):
    zero = jnp.zeros_like(up)
    return (
        jnp.where(low, down, zero),
        jnp.where(low, middle, jnp.where(even, down, zero)),
        jnp.where(low, up, jnp.where(even, middle, down)),
        jnp.where(low, zero, jnp.where(even, up, middle)),
        jnp.where(even, zero, up),
    )


def weigh(weights, reach):
    total = weights[0] * reach[0]
    for weight, value in zip(weights[1:], reach[1:]):
        total = total + weight * value
    return total


def roll_kernel(
    own,
    from_m1,
    from_m2,
    from_p1,
    payoff,
    positions,
    offsets,
    one,
    two,
    vol,
    out,
    sums,
    table,
    steps_k,
    nodes_k,
):
    me = lax.axis_index("bump")
    before, after = halos(one, two)
    sources = (own, from_m1, from_m2, from_p1)
    turns = (0, WORKERS - 1, WORKERS - 2, 1)
    turned = jnp.transpose(offsets[...].astype(jnp.float32))
    steps_k[8 : 8 + ROWS, :] = jnp.repeat(turned, ROWS // LANES, axis=0)
    steps_k[0:8, :] = jnp.transpose(before[2 * STEPS : HALO, 0:8])
    steps_k[8 + ROWS :, :] = jnp.transpose(after[2 * STEPS : HALO, 0:8])
    start = pl.multiple_of(me * CHUNK, CHUNK)
    part = jnp.concatenate(
        [
            steps_k[pl.ds(start + 8, CHUNK + 1), :],
            jnp.zeros((PADDED - CHUNK - 2, STEPS), jnp.float32),
            steps_k[pl.ds(start + 7, 1), :],
        ]
    )
    for s in range(STEPS):
        nodes_k[s] = jnp.broadcast_to(part[:, s : s + 1], (PADDED, LANES))
    above = payoff[pl.ds(pl.multiple_of(jnp.minimum(start + CHUNK, ROWS - 8), 8), 8), :]
    below = payoff[pl.ds(pl.multiple_of(jnp.maximum(start - 8, 0), 8), 8), :]
    values = jnp.concatenate(
        [
            payoff[pl.ds(start, CHUNK), :],
            jnp.where(me == WORKERS - 1, after[LOCAL_ROWS : LOCAL_ROWS + 1, :], above[0:1, :]),
            jnp.zeros((PADDED - CHUNK - 2, LANES), jnp.float32),
            jnp.where(me == 0, before[LOCAL_ROWS : LOCAL_ROWS + 1, :], below[7:8, :]),
        ]
    )
    gap = jnp.zeros((PADDED_PAIRS - CHUNK_PAIRS - 2 * LOCAL_STEPS, LANES), jnp.float32)
    for k in range(WORKERS):
        owner = lax.rem(me + turns[k], WORKERS)
        source = sources[k]
        for i in range(ROWS_PER_STEP):
            table[owner, i, :CHUNK_PAIRS, :] = source[i * CHUNK_PAIRS : (i + 1) * CHUNK_PAIRS, :]
            low = TABLE_ROWS + i * LOCAL_STEPS
            high = low + LOCAL_ROWS
            table[owner, i, CHUNK_PAIRS:, :] = jnp.concatenate(
                [source[high : high + LOCAL_STEPS, :], gap, source[low : low + LOCAL_STEPS, :]]
            )

    def rows(s, i):
        return table[s // LOCAL_STEPS, i, pl.ds(s % LOCAL_STEPS, PADDED, stride=LOCAL_STEPS), :]

    lane = lax.broadcasted_iota(jnp.int32, (PADDED, LANES), 1)
    slopes = {}
    for s in reversed(range(STEPS)):
        variance = vol[s] * vol[s]
        discount = rows(s, 0)
        up_slope = discount * rows(s, 2)
        down_slope = discount * rows(s, 4)
        up = discount * rows(s, 1) + variance * up_slope
        down = discount * rows(s, 3) + variance * down_slope
        low, even = nodes_k[s] < -0.5, nodes_k[s] < 0.5
        weights = spread(low, even, down, discount - up - down, up)
        slope_weights = spread(low, even, down_slope, -(up_slope + down_slope), up_slope)
        for q in list(slopes):
            reach = [shifted(slopes[q], m, lane) for m in range(-2, 3)]
            slopes[q] = weigh(weights, reach)
        reach = [shifted(values, m, lane) for m in range(-2, 3)]
        slopes[s] = weigh(slope_weights, reach)
        values = weigh(weights, reach)
    out[0:CHUNK, :] = values[0:CHUNK]
    weight = positions[pl.ds(start, CHUNK), :]
    lane8 = lax.broadcasted_iota(jnp.int32, (8, LANES), 1)
    held = jnp.zeros((8, LANES), jnp.float32)
    for s in range(STEPS):
        slope = slopes[s][0:CHUNK]
        out[(s + 1) * CHUNK : (s + 2) * CHUNK, :] = slope
        total = jnp.sum(jnp.sum(weight * slope, axis=0, keepdims=True), axis=1, keepdims=True)
        held = jnp.where(lane8 == s, total, held)
    sums[...] = jnp.broadcast_to(held[0:1, :], sums.shape)


def roll_back(messages, payoff, positions, offsets, one, two, vol, groups):
    return pl.pallas_call(
        roll_kernel,
        out_shape=(
            jax.ShapeDtypeStruct((VALUES, LANES), jnp.float32),
            jax.ShapeDtypeStruct((groups, LANES), jnp.float32),
        ),
        in_specs=[vmem()] * (WORKERS + 5) + [smem()],
        out_specs=(vmem(), vmem()),
        scratch_shapes=[
            pltpu.VMEM((WORKERS, ROWS_PER_STEP, PADDED_PAIRS, LANES), jnp.float32),
            pltpu.VMEM((ROWS + 16, STEPS), jnp.float32),
            pltpu.VMEM((STEPS, PADDED, LANES), jnp.float32),
        ],
        compiler_params=params(),
        name="roll_back",
    )(*messages, payoff, positions, offsets, one, two, vol)


def build(source, tile_rows, rate, bucket, bump):
    base = source[0:CHUNK, :]
    for b in range(CURVES):
        gain = bump[b] * rate[b]
        slope = source[pl.ds(pl.multiple_of((bucket[b] + 1) * CHUNK, CHUNK), CHUNK), :]
        tile_rows[b // 8, pl.ds(b % 8, CHUNK, stride=8), :] = base + gain * slope


def write(built, out, chunk, sems):
    stores = []
    for tile in range(CURVES // 8):
        rows = pl.ds(pl.multiple_of(chunk * CHUNK * 8, CHUNK * 8), CHUNK * 8)
        stores.append(pltpu.make_async_copy(built.at[tile], out.at[tile, rows, :], sems.at[tile]))
        stores[-1].start()
    return stores


def expand_kernel(own, from_m1, from_m2, from_p1, vol, bucket, bump, out, rate, built, done):
    me = lax.axis_index("bump")
    for b in range(CURVES):
        rate[b] = 2.0 * vol[bucket[b]] + bump[b]
    stores = []
    for k, (source, turn) in enumerate(((own, 0), (from_m1, 3), (from_m2, 2), (from_p1, 1))):
        build(source, built.at[k], rate, bucket, bump)
        stores += write(built.at[k], out, lax.rem(me + turn, WORKERS), done.at[k])
    for store in stores:
        store.wait()


def expand(parts, vol, bucket, bump):
    tiles = CURVES // 8
    laid, rate = pl.pallas_call(
        expand_kernel,
        out_shape=(
            jax.ShapeDtypeStruct((tiles, ROWS * 8, LANES), jnp.float32),
            jax.ShapeDtypeStruct((CURVES,), jnp.float32),
        ),
        in_specs=[vmem()] * WORKERS + [smem()] * 3,
        out_specs=(anywhere(), smem()),
        scratch_shapes=[
            pltpu.VMEM((WORKERS, tiles, CHUNK * 8, LANES), jnp.float32),
            pltpu.SemaphoreType.DMA((WORKERS, tiles)),
        ],
        compiler_params=params(),
        cost_estimate=EXPAND_COST,
        name="expand",
    )(*parts, vol, bucket, bump)
    curves = laid.reshape(tiles, ROWS, 8, LANES).transpose(0, 2, 1, 3)
    return curves.reshape(CURVES, ROWS * LANES), rate


def total_kernel(shared, out):
    out[...] = jnp.broadcast_to(jnp.sum(shared[...], axis=0, keepdims=True), out.shape)


def total(shared):
    return pl.pallas_call(
        total_kernel,
        out_shape=jax.ShapeDtypeStruct((8, LANES), jnp.float32),
        in_specs=[vmem()],
        out_specs=vmem(),
        compiler_params=params(),
        name="total",
    )(shared)


def vega_kernel(own, from_m1, from_m2, from_p1, bucket, rate, vega):
    totals = own[...] + from_m1[...] + from_m2[...] + from_p1[...]
    lane = lax.broadcasted_iota(jnp.int32, (8, LANES), 1)
    row = lax.broadcasted_iota(jnp.int32, (8, LANES), 0)
    line = jnp.zeros((1, LANES), jnp.float32)
    for tile in range(CURVES // 8):
        picked = jnp.zeros((8, LANES), jnp.float32)
        for r in range(8):
            b = tile * 8 + r
            hit = jnp.logical_and(row == r, lane == bucket[b])
            picked = jnp.where(hit, rate[b] * totals, picked)
        entry = jnp.sum(picked, axis=1, keepdims=True)
        line += jnp.sum(
            jnp.where(lane == row + tile * 8, entry, 0.0), axis=0, keepdims=True
        )
    vega[...] = line[:, :CURVES]


def vegas(parts, bucket, rate):
    return pl.pallas_call(
        vega_kernel,
        out_shape=jax.ShapeDtypeStruct((1, CURVES), jnp.float32),
        in_specs=[vmem()] * WORKERS + [smem(), smem()],
        out_specs=vmem(),
        compiler_params=params(),
        name="vegas",
    )(*parts, bucket, rate).reshape(CURVES)


def rotated(by):
    return [(i, (i + by) % WORKERS) for i in range(WORKERS)]


def exchanged(array, axis):
    return (array,) + tuple(lax.ppermute(array, axis, rotated(by)) for by in (1, 2, -1))


def on_device(payoff, positions, tables, offsets, vol_curve, bucket, bump_size):
    groups = lax.axis_size(NODE_AXES)
    with_next = [(i, i ^ 1) for i in range(groups)]
    with_last = [(i, (i + (1 if i % 2 else groups - 1)) % groups) for i in range(groups)]
    payoff_rows = payoff.reshape(ROWS, LANES)
    tables = tables.transpose(1, 0, 2).reshape(ROWS_PER_STEP, LOCAL_STEPS, ROWS, LANES)
    tables = tables.transpose(0, 2, 1, 3).reshape(ROWS_PER_STEP, PAIRS, LANES)
    one, two = edges(tables, payoff_rows, offsets)
    one = lax.ppermute(one, NODE_AXES, with_next)
    two = lax.ppermute(two, NODE_AXES, with_last)
    held, payoff_rows, position_rows = load(tables, payoff_rows, positions.reshape(ROWS, LANES))
    messages = pack(held, one, two)
    received = (
        messages[0],
        lax.ppermute(messages[1], "bump", rotated(1)),
        lax.ppermute(messages[2], "bump", rotated(2)),
        lax.ppermute(messages[3], "bump", rotated(-1)),
    )
    arrays, sums = roll_back(
        received, payoff_rows, position_rows, offsets, one, two, vol_curve, groups
    )
    bumped_values, rate = expand(exchanged(arrays, "bump"), vol_curve, bucket, bump_size)
    shared = lax.all_to_all(
        sums.reshape(groups, 1, LANES), NODE_AXES, split_axis=0, concat_axis=0, tiled=True
    )
    shared, rate = lax.optimization_barrier((shared, rate))
    totals = exchanged(total(shared.reshape(groups, LANES)), "bump")
    return (bumped_values, vegas(totals, bucket, rate))


def solution(mesh):
    in_specs = (
        P(("nx", "ny")),
        P(("nx", "ny")),
        P("bump", None, ("nx", "ny")),
        P(None, ("nx", "ny")),
        P(),
        P("bump"),
        P("bump"),
    )
    out_specs = (P("bump", ("nx", "ny")), P("bump"))
    return jax.shard_map(
        on_device, mesh=mesh, in_specs=in_specs, out_specs=out_specs, check_vma=False
    )
```

```python
import jax
import jax.numpy as jnp
from jax import lax
from jax.experimental import pallas as pl
from jax.experimental.pallas import tpu as pltpu
from jax.sharding import PartitionSpec as P

NODE_AXES = ("nx", "ny")
ALL_AXES = ("bump", "nx", "ny")
LANES = 128
ROWS_PER_STEP = 5
STEPS = 8
WORKERS = 4
LOCAL_STEPS = STEPS // WORKERS
LOCAL_ROWS = LOCAL_STEPS * ROWS_PER_STEP
CURVES = 16
VMEM_LIMIT = 48 * 1024 * 1024

ROWS = 256
CHUNK = ROWS // WORKERS
PADDED = CHUNK + 8
PAIRS = LOCAL_STEPS * ROWS
CHUNK_PAIRS = LOCAL_STEPS * CHUNK
PADDED_PAIRS = LOCAL_STEPS * PADDED
TABLE_ROWS = LOCAL_ROWS * CHUNK
GHOST_ROWS = 24
MESSAGE = TABLE_ROWS + GHOST_ROWS
HALO = 24
VALUES = (STEPS + 1) * CHUNK
HALF = VALUES // 2

EXPAND_COST = pl.CostEstimate(flops=100_000_000, bytes_accessed=100_000_000, transcendentals=0)

VMEM = pltpu.MemorySpace.VMEM
SMEM = pltpu.MemorySpace.SMEM


def params(limit=VMEM_LIMIT):
    return pltpu.CompilerParams(vmem_limit_bytes=limit)


def vmem():
    return pl.BlockSpec(memory_space=VMEM)


def smem():
    return pl.BlockSpec(memory_space=SMEM)


def anywhere():
    return pl.BlockSpec(memory_space=pl.ANY)


def in_hbm(array):
    return pltpu.with_memory_space_constraint(array, pltpu.HBM)


def hbm():
    return pl.BlockSpec(memory_space=pltpu.HBM)


def on_even_group():
    return lax.rem(lax.axis_index("ny"), 2) == 0


def halos(one, two):
    even = on_even_group()
    return jnp.where(even, two[...], one[...]), jnp.where(even, one[...], two[...])


def edges_kernel(tables, payoff, offsets, one, two, held, held_payoff, held_offsets, ends, sem):
    copies = [pltpu.make_async_copy(offsets, held_offsets, sem.at[2, 0])]
    for side, pair, row in ((0, 0, 0), (1, PAIRS - 8, ROWS - 8)):
        copies.append(
            pltpu.make_async_copy(tables.at[:, pl.ds(pair, 8), :], held.at[side], sem.at[0, side])
        )
        copies.append(
            pltpu.make_async_copy(
                payoff.at[pl.ds(row, 8), :], held_payoff.at[side], sem.at[1, side]
            )
        )
    for copy in copies:
        copy.start()
    for copy in copies:
        copy.wait()
    for side, row, lane in ((0, 0, 0), (1, 7, LANES - 1)):
        out = ends.at[side]
        pair = row * (8 - LOCAL_STEPS) // 7
        for i in range(ROWS_PER_STEP):
            out[i * LOCAL_STEPS : (i + 1) * LOCAL_STEPS, :] = held[
                side, i, pair : pair + LOCAL_STEPS, :
            ]
        out[LOCAL_ROWS : 2 * STEPS, :] = jnp.broadcast_to(
            held_payoff[side, row : row + 1, :], (2 * STEPS - LOCAL_ROWS, LANES)
        )
        out[2 * STEPS : HALO, :] = jnp.broadcast_to(
            held_offsets[:, lane : lane + 1].astype(jnp.float32), (STEPS, LANES)
        )
    one[...] = jnp.where(on_even_group(), ends[1], ends[0])
    two[...] = jnp.where(on_even_group(), ends[0], ends[1])


def edges(tables, payoff_rows, offsets):
    shape = jax.ShapeDtypeStruct((HALO, LANES), jnp.float32)
    return pl.pallas_call(
        edges_kernel,
        out_shape=(shape, shape),
        in_specs=[hbm(), hbm(), hbm()],
        out_specs=(vmem(), vmem()),
        scratch_shapes=[
            pltpu.VMEM((2, ROWS_PER_STEP, 8, LANES), jnp.float32),
            pltpu.VMEM((2, 8, LANES), jnp.float32),
            pltpu.VMEM((STEPS, LANES), jnp.int32),
            pltpu.VMEM((2, HALO, LANES), jnp.float32),
            pltpu.SemaphoreType.DMA((3, 2)),
        ],
        compiler_params=params(),
        name="edges",
    )(*(in_hbm(array) for array in (tables, payoff_rows, offsets)))


def load_kernel(tables, payoff, positions, held, held_payoff, held_positions, sem):
    copies = [
        pltpu.make_async_copy(source, target, sem.at[i])
        for i, (source, target) in enumerate(
            ((tables, held), (payoff, held_payoff), (positions, held_positions))
        )
    ]
    for copy in copies:
        copy.start()
    for copy in copies:
        copy.wait()


def load(*arrays):
    return pl.pallas_call(
        load_kernel,
        out_shape=tuple(jax.ShapeDtypeStruct(array.shape, array.dtype) for array in arrays),
        in_specs=[hbm()] * len(arrays),
        out_specs=(vmem(),) * len(arrays),
        scratch_shapes=[pltpu.SemaphoreType.DMA((len(arrays),))],
        compiler_params=params(),
        cost_estimate=pl.CostEstimate(flops=0, bytes_accessed=6_000_000, transcendentals=0),
        name="load",
    )(*(in_hbm(array) for array in arrays))


def pack_kernel(tables, one, two, own, plus1, plus2, plus3):
    me = lax.axis_index("bump")
    before, after = halos(one, two)
    for k, out in ((1, plus1), (3, plus3), (2, plus2), (0, own)):
        chunk = lax.rem(me + k, WORKERS)
        below = lax.rem(chunk + WORKERS - 1, WORKERS)
        above = lax.rem(chunk + 1, WORKERS)
        start = pl.multiple_of(chunk * CHUNK_PAIRS, CHUNK_PAIRS)
        low = pl.multiple_of(below * CHUNK_PAIRS + CHUNK_PAIRS - 8, 8)
        high = pl.multiple_of(above * CHUNK_PAIRS, CHUNK_PAIRS)
        for i in range(ROWS_PER_STEP):
            out[i * CHUNK_PAIRS : (i + 1) * CHUNK_PAIRS, :] = tables[i, pl.ds(start, CHUNK_PAIRS), :]
            at = slice(i * LOCAL_STEPS, (i + 1) * LOCAL_STEPS)
            row = TABLE_ROWS + i * LOCAL_STEPS
            out[row : row + LOCAL_STEPS, :] = jnp.where(
                chunk == 0, before[at, :], tables[i, pl.ds(low, 8), :][8 - LOCAL_STEPS :]
            )
            row += LOCAL_ROWS
            out[row : row + LOCAL_STEPS, :] = jnp.where(
                chunk == WORKERS - 1, after[at, :], tables[i, pl.ds(high, 8), :][:LOCAL_STEPS]
            )
        out[TABLE_ROWS + 2 * LOCAL_ROWS :, :] = jnp.zeros(
            (GHOST_ROWS - 2 * LOCAL_ROWS, LANES), jnp.float32
        )


def pack(tables, one, two):
    shape = jax.ShapeDtypeStruct((MESSAGE, LANES), jnp.float32)
    return pl.pallas_call(
        pack_kernel,
        out_shape=(shape,) * WORKERS,
        in_specs=[vmem()] * 3,
        out_specs=(vmem(),) * WORKERS,
        compiler_params=params(),
        name="pack",
    )(tables, one, two)


def shifted(values, by, lane):
    if by == 0:
        return values
    turned = pltpu.roll(values, (-by) % LANES, 1)
    if by > 0:
        return jnp.where(lane < LANES - by, turned, pltpu.roll(turned, PADDED - 1, 0))
    return jnp.where(lane >= -by, turned, pltpu.roll(turned, 1, 0))


def spread(low, even, down, middle, up):
    zero = jnp.zeros_like(up)
    return (
        jnp.where(low, down, zero),
        jnp.where(low, middle, jnp.where(even, down, zero)),
        jnp.where(low, up, jnp.where(even, middle, down)),
        jnp.where(low, zero, jnp.where(even, up, middle)),
        jnp.where(even, zero, up),
    )


def weigh(weights, reach):
    total = weights[0] * reach[0]
    for weight, value in zip(weights[1:], reach[1:]):
        total = total + weight * value
    return total


def roll_kernel(
    own,
    from_m1,
    from_m2,
    from_p1,
    payoff,
    positions,
    offsets,
    one,
    two,
    vol,
    out,
    sums,
    table,
    steps_k,
    nodes_k,
):
    me = lax.axis_index("bump")
    before, after = halos(one, two)
    sources = (own, from_m1, from_m2, from_p1)
    turns = (0, WORKERS - 1, WORKERS - 2, 1)
    turned = jnp.transpose(offsets[...].astype(jnp.float32))
    steps_k[8 : 8 + ROWS, :] = jnp.repeat(turned, ROWS // LANES, axis=0)
    steps_k[0:8, :] = jnp.transpose(before[2 * STEPS : HALO, 0:8])
    steps_k[8 + ROWS :, :] = jnp.transpose(after[2 * STEPS : HALO, 0:8])
    start = pl.multiple_of(me * CHUNK, CHUNK)
    part = jnp.concatenate(
        [
            steps_k[pl.ds(start + 8, CHUNK + 1), :],
            jnp.zeros((PADDED - CHUNK - 2, STEPS), jnp.float32),
            steps_k[pl.ds(start + 7, 1), :],
        ]
    )
    for s in range(STEPS):
        nodes_k[s] = jnp.broadcast_to(part[:, s : s + 1], (PADDED, LANES))
    above = payoff[pl.ds(pl.multiple_of(jnp.minimum(start + CHUNK, ROWS - 8), 8), 8), :]
    below = payoff[pl.ds(pl.multiple_of(jnp.maximum(start - 8, 0), 8), 8), :]
    values = jnp.concatenate(
        [
            payoff[pl.ds(start, CHUNK), :],
            jnp.where(me == WORKERS - 1, after[LOCAL_ROWS : LOCAL_ROWS + 1, :], above[0:1, :]),
            jnp.zeros((PADDED - CHUNK - 2, LANES), jnp.float32),
            jnp.where(me == 0, before[LOCAL_ROWS : LOCAL_ROWS + 1, :], below[7:8, :]),
        ]
    )
    gap = jnp.zeros((PADDED_PAIRS - CHUNK_PAIRS - 2 * LOCAL_STEPS, LANES), jnp.float32)
    for k in range(WORKERS):
        owner = lax.rem(me + turns[k], WORKERS)
        source = sources[k]
        for i in range(ROWS_PER_STEP):
            table[owner, i, :CHUNK_PAIRS, :] = source[i * CHUNK_PAIRS : (i + 1) * CHUNK_PAIRS, :]
            low = TABLE_ROWS + i * LOCAL_STEPS
            high = low + LOCAL_ROWS
            table[owner, i, CHUNK_PAIRS:, :] = jnp.concatenate(
                [source[high : high + LOCAL_STEPS, :], gap, source[low : low + LOCAL_STEPS, :]]
            )

    def rows(s, i):
        return table[s // LOCAL_STEPS, i, pl.ds(s % LOCAL_STEPS, PADDED, stride=LOCAL_STEPS), :]

    lane = lax.broadcasted_iota(jnp.int32, (PADDED, LANES), 1)
    slopes = {}
    for s in reversed(range(STEPS)):
        variance = vol[s] * vol[s]
        discount = rows(s, 0)
        up_slope = discount * rows(s, 2)
        down_slope = discount * rows(s, 4)
        up = discount * rows(s, 1) + variance * up_slope
        down = discount * rows(s, 3) + variance * down_slope
        low, even = nodes_k[s] < -0.5, nodes_k[s] < 0.5
        weights = spread(low, even, down, discount - up - down, up)
        slope_weights = spread(low, even, down_slope, -(up_slope + down_slope), up_slope)
        for q in list(slopes):
            reach = [shifted(slopes[q], m, lane) for m in range(-2, 3)]
            slopes[q] = weigh(weights, reach)
        reach = [shifted(values, m, lane) for m in range(-2, 3)]
        slopes[s] = weigh(slope_weights, reach)
        values = weigh(weights, reach)
    out[0:CHUNK, :] = values[0:CHUNK]
    weight = positions[pl.ds(start, CHUNK), :]
    lines = []
    for s in range(STEPS):
        slope = slopes[s][0:CHUNK]
        out[(s + 1) * CHUNK : (s + 2) * CHUNK, :] = slope
        lines.append(jnp.sum(weight * slope, axis=0, keepdims=True))
    totals = jnp.sum(jnp.concatenate(lines), axis=1, keepdims=True)
    step = lax.broadcasted_iota(jnp.int32, (STEPS, LANES), 0)
    own_lane = lax.broadcasted_iota(jnp.int32, (STEPS, LANES), 1) == step
    line = jnp.sum(jnp.where(own_lane, totals, 0.0), axis=0, keepdims=True)
    sums[...] = jnp.broadcast_to(line, sums.shape)


def roll_back(messages, payoff, positions, offsets, one, two, vol, peers):
    return pl.pallas_call(
        roll_kernel,
        out_shape=(
            jax.ShapeDtypeStruct((VALUES, LANES), jnp.float32),
            jax.ShapeDtypeStruct((peers, LANES), jnp.float32),
        ),
        in_specs=[vmem()] * (WORKERS + 5) + [smem()],
        out_specs=(vmem(), vmem()),
        scratch_shapes=[
            pltpu.VMEM((WORKERS, ROWS_PER_STEP, PADDED_PAIRS, LANES), jnp.float32),
            pltpu.VMEM((ROWS + 16, STEPS), jnp.float32),
            pltpu.VMEM((STEPS, PADDED, LANES), jnp.float32),
        ],
        compiler_params=params(),
        name="roll_back",
    )(*messages, payoff, positions, offsets, one, two, vol)


def build(source, tile_rows, rate, bucket, bump):
    base = source[0:CHUNK, :]
    for b in range(CURVES):
        gain = bump[b] * rate[b]
        slope = source[pl.ds(pl.multiple_of((bucket[b] + 1) * CHUNK, CHUNK), CHUNK), :]
        tile_rows[b // 8, pl.ds(b % 8, CHUNK, stride=8), :] = base + gain * slope


def write(built, out, chunk, sems):
    stores = []
    for tile in range(CURVES // 8):
        rows = pl.ds(pl.multiple_of(chunk * CHUNK * 8, CHUNK * 8), CHUNK * 8)
        stores.append(pltpu.make_async_copy(built.at[tile], out.at[tile, rows, :], sems.at[tile]))
        stores[-1].start()
    return stores


def rates(vol, bucket, bump):
    return [2.0 * vol[bucket[b]] + bump[b] for b in range(CURVES)]


def expand_chunks(parts, vol, bucket, bump, out, built, done):
    me = lax.axis_index("bump")
    rate = rates(vol, bucket, bump)
    stores = []
    for k, (source, turn) in enumerate(parts):
        build(source, built.at[k], rate, bucket, bump)
        stores += write(built.at[k], out, lax.rem(me + turn, WORKERS), done.at[k])
    for store in stores:
        store.wait()


def expand_kernel(own, from_m1, from_p1, vol, bucket, bump, out, built, done):
    parts = ((own, 0), (from_m1, WORKERS - 1), (from_p1, 1))
    expand_chunks(parts, vol, bucket, bump, out, built, done)


def scratch(chunks):
    tiles = CURVES // 8
    return [
        pltpu.VMEM((chunks, tiles, CHUNK * 8, LANES), jnp.float32),
        pltpu.SemaphoreType.DMA((chunks, tiles)),
    ]


def expand(own, from_m1, from_p1, vol, bucket, bump):
    return pl.pallas_call(
        expand_kernel,
        out_shape=jax.ShapeDtypeStruct((CURVES // 8, ROWS * 8, LANES), jnp.float32),
        in_specs=[vmem()] * 3 + [smem()] * 3,
        out_specs=anywhere(),
        scratch_shapes=scratch(3),
        compiler_params=params(),
        cost_estimate=EXPAND_COST,
        name="expand",
    )(own, from_m1, from_p1, vol, bucket, bump)


def complete_kernel(low, high, vol, bucket, bump, started, out, picks, joined, built, done):
    del started
    rate = rates(vol, bucket, bump)
    row = lax.broadcasted_iota(jnp.int32, (CURVES, LANES), 0)
    lane = lax.broadcasted_iota(jnp.int32, (CURVES, LANES), 1)
    pick = jnp.zeros((CURVES, LANES), jnp.float32)
    for b in range(CURVES):
        pick = jnp.where(jnp.logical_and(row == b, lane == bucket[b]), rate[b], pick)
    picks[...] = pick
    joined[0:HALF, :] = low[...]
    joined[HALF:, :] = high[...]
    expand_chunks(((joined, WORKERS - 2),), vol, bucket, bump, out, built, done)


def complete(low, high, vol, bucket, bump, started):
    tiles = CURVES // 8
    laid, picks = pl.pallas_call(
        complete_kernel,
        out_shape=(
            jax.ShapeDtypeStruct(started.shape, started.dtype),
            jax.ShapeDtypeStruct((CURVES, LANES), jnp.float32),
        ),
        in_specs=[vmem()] * 2 + [smem()] * 3 + [anywhere()],
        out_specs=(anywhere(), vmem()),
        scratch_shapes=[pltpu.VMEM((VALUES, LANES), jnp.float32)] + scratch(1),
        input_output_aliases={5: 0},
        compiler_params=params(),
        cost_estimate=EXPAND_COST,
        name="complete",
    )(low, high, vol, bucket, bump, started)
    curves = laid.reshape(tiles, ROWS, 8, LANES).transpose(0, 2, 1, 3)
    return curves.reshape(CURVES, ROWS * LANES), picks


def vega_kernel(shared, picks, vega):
    totals = jnp.sum(shared[...], axis=0, keepdims=True)
    entry = jnp.sum(picks[...] * totals, axis=1, keepdims=True)
    row = lax.broadcasted_iota(jnp.int32, (CURVES, LANES), 0)
    lane = lax.broadcasted_iota(jnp.int32, (CURVES, LANES), 1)
    line = jnp.sum(jnp.where(lane == row, entry, 0.0), axis=0, keepdims=True)
    vega[...] = line[:, :CURVES]


def vegas(shared, picks):
    return pl.pallas_call(
        vega_kernel,
        out_shape=jax.ShapeDtypeStruct((1, CURVES), jnp.float32),
        in_specs=[vmem(), vmem()],
        out_specs=vmem(),
        compiler_params=params(),
        name="vegas",
    )(shared, picks).reshape(CURVES)


def rotated(by):
    return [(i, (i + by) % WORKERS) for i in range(WORKERS)]


def on_device(payoff, positions, tables, offsets, vol_curve, bucket, bump_size):
    groups = lax.axis_size(NODE_AXES)
    with_next = [(i, i ^ 1) for i in range(groups)]
    with_last = [(i, (i + (1 if i % 2 else groups - 1)) % groups) for i in range(groups)]
    payoff_rows = payoff.reshape(ROWS, LANES)
    tables = tables.transpose(1, 0, 2).reshape(ROWS_PER_STEP, LOCAL_STEPS, ROWS, LANES)
    tables = tables.transpose(0, 2, 1, 3).reshape(ROWS_PER_STEP, PAIRS, LANES)
    one, two = edges(tables, payoff_rows, offsets)
    one = lax.ppermute(one, NODE_AXES, with_next)
    two = lax.ppermute(two, NODE_AXES, with_last)
    held, payoff_rows, position_rows = load(tables, payoff_rows, positions.reshape(ROWS, LANES))
    messages = pack(held, one, two)
    received = (
        messages[0],
        lax.ppermute(messages[1], "bump", rotated(1)),
        lax.ppermute(messages[2], "bump", rotated(2)),
        lax.ppermute(messages[3], "bump", rotated(-1)),
    )
    peers = lax.axis_size(ALL_AXES)
    arrays, sums = roll_back(
        received, payoff_rows, position_rows, offsets, one, two, vol_curve, peers
    )
    from_m1 = lax.ppermute(arrays, "bump", rotated(1))
    from_p1 = lax.ppermute(arrays, "bump", rotated(-1))
    low = lax.ppermute(from_m1[:HALF], "bump", rotated(1))
    high = lax.ppermute(from_p1[HALF:], "bump", rotated(-1))
    started = expand(arrays, from_m1, from_p1, vol_curve, bucket, bump_size)
    bumped_values, picks = complete(low, high, vol_curve, bucket, bump_size, started)
    shared = lax.all_to_all(
        sums.reshape(peers, 1, LANES), ALL_AXES, split_axis=0, concat_axis=0, tiled=True
    )
    return (bumped_values, vegas(shared.reshape(peers, LANES), picks))


def solution(mesh):
    in_specs = (
        P(("nx", "ny")),
        P(("nx", "ny")),
        P("bump", None, ("nx", "ny")),
        P(None, ("nx", "ny")),
        P(),
        P("bump"),
        P("bump"),
    )
    out_specs = (P("bump", ("nx", "ny")), P("bump"))
    return jax.shard_map(
        on_device, mesh=mesh, in_specs=in_specs, out_specs=out_specs, check_vma=False
    )
```

```python
import jax
import jax.numpy as jnp
from jax import lax
from jax.experimental import pallas as pl
from jax.experimental.pallas import tpu as pltpu
from jax.sharding import PartitionSpec as P

NODE_AXES = ("nx", "ny")
ALL_AXES = ("bump", "nx", "ny")
LANES = 128
ROWS_PER_STEP = 5
STEPS = 8
WORKERS = 4
LOCAL_STEPS = STEPS // WORKERS
LOCAL_ROWS = LOCAL_STEPS * ROWS_PER_STEP
CURVES = 16
VMEM_LIMIT = 48 * 1024 * 1024

ROWS = 256
CHUNK = ROWS // WORKERS
PADDED = CHUNK + 8
PAIRS = LOCAL_STEPS * ROWS
CHUNK_PAIRS = LOCAL_STEPS * CHUNK
PADDED_PAIRS = LOCAL_STEPS * PADDED
TABLE_ROWS = LOCAL_ROWS * CHUNK
GHOST_ROWS = 24
MESSAGE = TABLE_ROWS + GHOST_ROWS
HALO = 24
VALUES = (STEPS + 1) * CHUNK
HALF = VALUES // 2

EXPAND_COST = pl.CostEstimate(flops=100_000_000, bytes_accessed=100_000_000, transcendentals=0)

VMEM = pltpu.MemorySpace.VMEM
SMEM = pltpu.MemorySpace.SMEM


def params(limit=VMEM_LIMIT):
    return pltpu.CompilerParams(vmem_limit_bytes=limit)


def vmem():
    return pl.BlockSpec(memory_space=VMEM)


def smem():
    return pl.BlockSpec(memory_space=SMEM)


def anywhere():
    return pl.BlockSpec(memory_space=pl.ANY)


def in_hbm(array):
    return pltpu.with_memory_space_constraint(array, pltpu.HBM)


def hbm():
    return pl.BlockSpec(memory_space=pltpu.HBM)


def on_even_group():
    return lax.rem(lax.axis_index("ny"), 2) == 0


def halos(one, two):
    even = on_even_group()
    return jnp.where(even, two[...], one[...]), jnp.where(even, one[...], two[...])


def pack_one(tables, k, out, before, after):
    chunk = lax.rem(lax.axis_index("bump") + k, WORKERS)
    start = pl.multiple_of(chunk * CHUNK_PAIRS, CHUNK_PAIRS)
    low = pl.multiple_of(lax.rem(start + PAIRS - 8, PAIRS), 8)
    high = pl.multiple_of(lax.rem(start + CHUNK_PAIRS, PAIRS), CHUNK_PAIRS)
    for i in range(ROWS_PER_STEP):
        out[i * CHUNK_PAIRS : (i + 1) * CHUNK_PAIRS, :] = tables[i, pl.ds(start, CHUNK_PAIRS), :]
        at = slice(i * LOCAL_STEPS, (i + 1) * LOCAL_STEPS)
        beside = tables[i, pl.ds(low, 8), :][8 - LOCAL_STEPS :]
        if before is not None:
            beside = jnp.where(chunk == 0, before[at, :], beside)
        row = TABLE_ROWS + i * LOCAL_STEPS
        out[row : row + LOCAL_STEPS, :] = beside
        beside = tables[i, pl.ds(high, 8), :][:LOCAL_STEPS]
        if after is not None:
            beside = jnp.where(chunk == WORKERS - 1, after[at, :], beside)
        row += LOCAL_ROWS
        out[row : row + LOCAL_STEPS, :] = beside
    out[TABLE_ROWS + 2 * LOCAL_ROWS :, :] = jnp.zeros(
        (GHOST_ROWS - 2 * LOCAL_ROWS, LANES), jnp.float32
    )


def first_kernel(
    tables,
    payoff,
    positions,
    offsets,
    held_tables,
    held_payoff,
    held_positions,
    held_offsets,
    plus2,
    one,
    two,
    far,
    ends,
    sem,
):
    held = (held_tables, held_payoff, held_positions, held_offsets)
    copies = [
        pltpu.make_async_copy(source, target, sem.at[i])
        for i, (source, target) in enumerate(zip((tables, payoff, positions, offsets), held))
    ]
    for copy in copies:
        copy.start()
    for copy in copies:
        copy.wait()
    pack_one(held_tables, 2, plus2, None, None)
    for side, pair, row, lane in ((0, 0, 0, 0), (1, PAIRS - LOCAL_STEPS, ROWS - 1, LANES - 1)):
        out = ends.at[side]
        for i in range(ROWS_PER_STEP):
            out[i * LOCAL_STEPS : (i + 1) * LOCAL_STEPS, :] = held_tables[
                i, pair : pair + LOCAL_STEPS, :
            ]
        out[LOCAL_ROWS : 2 * STEPS, :] = jnp.broadcast_to(
            held_payoff[row : row + 1, :], (2 * STEPS - LOCAL_ROWS, LANES)
        )
        out[2 * STEPS : HALO, :] = jnp.broadcast_to(
            held_offsets[:, lane : lane + 1].astype(jnp.float32), (STEPS, LANES)
        )
    one[...] = jnp.where(on_even_group(), ends[1], ends[0])
    two[...] = jnp.where(on_even_group(), ends[0], ends[1])
    far[...] = jnp.where(lax.axis_index("bump") == WORKERS // 2, ends[1], ends[0])


def first(*arrays):
    same = tuple(jax.ShapeDtypeStruct(array.shape, array.dtype) for array in arrays)
    message = jax.ShapeDtypeStruct((MESSAGE, LANES), jnp.float32)
    halo = jax.ShapeDtypeStruct((HALO, LANES), jnp.float32)
    return pl.pallas_call(
        first_kernel,
        out_shape=same + (message, halo, halo, halo),
        in_specs=[hbm()] * len(arrays),
        out_specs=(vmem(),) * (len(arrays) + 4),
        scratch_shapes=[
            pltpu.VMEM((2, HALO, LANES), jnp.float32),
            pltpu.SemaphoreType.DMA((len(arrays),)),
        ],
        compiler_params=params(),
        name="first",
    )(*(in_hbm(array) for array in arrays))


def pack_near_kernel(tables, one, two, own, plus1, plus3):
    before, after = halos(one, two)
    for k, out in ((1, plus1), (3, plus3), (0, own)):
        pack_one(tables, k, out, before, after)


def pack_near(tables, one, two):
    shape = jax.ShapeDtypeStruct((MESSAGE, LANES), jnp.float32)
    return pl.pallas_call(
        pack_near_kernel,
        out_shape=(shape,) * 3,
        in_specs=[vmem()] * 3,
        out_specs=(vmem(),) * 3,
        compiler_params=params(),
        name="pack",
    )(tables, one, two)


def shifted(values, by, lane):
    if by == 0:
        return values
    turned = pltpu.roll(values, (-by) % LANES, 1)
    if by > 0:
        return jnp.where(lane < LANES - by, turned, pltpu.roll(turned, PADDED - 1, 0))
    return jnp.where(lane >= -by, turned, pltpu.roll(turned, 1, 0))


def spread(low, even, down, middle, up):
    zero = jnp.zeros_like(up)
    return (
        jnp.where(low, down, zero),
        jnp.where(low, middle, jnp.where(even, down, zero)),
        jnp.where(low, up, jnp.where(even, middle, down)),
        jnp.where(low, zero, jnp.where(even, up, middle)),
        jnp.where(even, zero, up),
    )


def weigh(weights, reach):
    total = weights[0] * reach[0]
    for weight, value in zip(weights[1:], reach[1:]):
        total = total + weight * value
    return total


def roll_kernel(
    own,
    from_m1,
    from_m2,
    from_p1,
    payoff,
    positions,
    offsets,
    one,
    two,
    far,
    vol,
    out,
    sums,
    table,
    steps_k,
    nodes_k,
):
    me = lax.axis_index("bump")
    before, after = halos(one, two)
    sources = (own, from_m1, from_m2, from_p1)
    turns = (0, WORKERS - 1, WORKERS - 2, 1)
    turned = jnp.transpose(offsets[...].astype(jnp.float32))
    steps_k[8 : 8 + ROWS, :] = jnp.repeat(turned, ROWS // LANES, axis=0)
    steps_k[0:8, :] = jnp.transpose(before[2 * STEPS : HALO, 0:8])
    steps_k[8 + ROWS :, :] = jnp.transpose(after[2 * STEPS : HALO, 0:8])
    start = pl.multiple_of(me * CHUNK, CHUNK)
    part = jnp.concatenate(
        [
            steps_k[pl.ds(start + 8, CHUNK + 1), :],
            jnp.zeros((PADDED - CHUNK - 2, STEPS), jnp.float32),
            steps_k[pl.ds(start + 7, 1), :],
        ]
    )
    for s in range(STEPS):
        nodes_k[s] = jnp.broadcast_to(part[:, s : s + 1], (PADDED, LANES))
    above = payoff[pl.ds(pl.multiple_of(jnp.minimum(start + CHUNK, ROWS - 8), 8), 8), :]
    below = payoff[pl.ds(pl.multiple_of(jnp.maximum(start - 8, 0), 8), 8), :]
    values = jnp.concatenate(
        [
            payoff[pl.ds(start, CHUNK), :],
            jnp.where(me == WORKERS - 1, after[LOCAL_ROWS : LOCAL_ROWS + 1, :], above[0:1, :]),
            jnp.zeros((PADDED - CHUNK - 2, LANES), jnp.float32),
            jnp.where(me == 0, before[LOCAL_ROWS : LOCAL_ROWS + 1, :], below[7:8, :]),
        ]
    )
    gap = jnp.zeros((PADDED_PAIRS - CHUNK_PAIRS - 2 * LOCAL_STEPS, LANES), jnp.float32)
    for k in range(WORKERS):
        owner = lax.rem(me + turns[k], WORKERS)
        source = sources[k]
        for i in range(ROWS_PER_STEP):
            table[owner, i, :CHUNK_PAIRS, :] = source[i * CHUNK_PAIRS : (i + 1) * CHUNK_PAIRS, :]
            at = slice(i * LOCAL_STEPS, (i + 1) * LOCAL_STEPS)
            low = TABLE_ROWS + i * LOCAL_STEPS
            high = low + LOCAL_ROWS
            ahead = source[low : low + LOCAL_STEPS, :]
            behind = source[high : high + LOCAL_STEPS, :]
            if k == 2:
                ahead = jnp.where(me == 0, far[at, :], ahead)
                behind = jnp.where(me == WORKERS - 1, far[at, :], behind)
            table[owner, i, CHUNK_PAIRS:, :] = jnp.concatenate([behind, gap, ahead])

    def rows(s, i):
        return table[s // LOCAL_STEPS, i, pl.ds(s % LOCAL_STEPS, PADDED, stride=LOCAL_STEPS), :]

    lane = lax.broadcasted_iota(jnp.int32, (PADDED, LANES), 1)
    slopes = {}
    for s in reversed(range(STEPS)):
        variance = vol[s] * vol[s]
        discount = rows(s, 0)
        up_slope = discount * rows(s, 2)
        down_slope = discount * rows(s, 4)
        up = discount * rows(s, 1) + variance * up_slope
        down = discount * rows(s, 3) + variance * down_slope
        low, even = nodes_k[s] < -0.5, nodes_k[s] < 0.5
        weights = spread(low, even, down, discount - up - down, up)
        slope_weights = spread(low, even, down_slope, -(up_slope + down_slope), up_slope)
        for q in list(slopes):
            reach = [shifted(slopes[q], m, lane) for m in range(-2, 3)]
            slopes[q] = weigh(weights, reach)
        reach = [shifted(values, m, lane) for m in range(-2, 3)]
        slopes[s] = weigh(slope_weights, reach)
        values = weigh(weights, reach)
    out[0:CHUNK, :] = values[0:CHUNK]
    weight = positions[pl.ds(start, CHUNK), :]
    lines = []
    for s in range(STEPS):
        slope = slopes[s][0:CHUNK]
        out[(s + 1) * CHUNK : (s + 2) * CHUNK, :] = slope
        lines.append(jnp.sum(weight * slope, axis=0, keepdims=True))
    totals = jnp.sum(jnp.concatenate(lines), axis=1, keepdims=True)
    step = lax.broadcasted_iota(jnp.int32, (STEPS, LANES), 0)
    own_lane = lax.broadcasted_iota(jnp.int32, (STEPS, LANES), 1) == step
    line = jnp.sum(jnp.where(own_lane, totals, 0.0), axis=0, keepdims=True)
    sums[...] = jnp.broadcast_to(line, sums.shape)


def roll_back(messages, payoff, positions, offsets, one, two, far, vol, peers):
    return pl.pallas_call(
        roll_kernel,
        out_shape=(
            jax.ShapeDtypeStruct((VALUES, LANES), jnp.float32),
            jax.ShapeDtypeStruct((peers, LANES), jnp.float32),
        ),
        in_specs=[vmem()] * (WORKERS + 6) + [smem()],
        out_specs=(vmem(), vmem()),
        scratch_shapes=[
            pltpu.VMEM((WORKERS, ROWS_PER_STEP, PADDED_PAIRS, LANES), jnp.float32),
            pltpu.VMEM((ROWS + 16, STEPS), jnp.float32),
            pltpu.VMEM((STEPS, PADDED, LANES), jnp.float32),
        ],
        compiler_params=params(),
        name="roll_back",
    )(*messages, payoff, positions, offsets, one, two, far, vol)


def build(source, tile_rows, rate, bucket, bump):
    base = source[0:CHUNK, :]
    for b in range(CURVES):
        gain = bump[b] * rate[b]
        slope = source[pl.ds(pl.multiple_of((bucket[b] + 1) * CHUNK, CHUNK), CHUNK), :]
        tile_rows[b // 8, pl.ds(b % 8, CHUNK, stride=8), :] = base + gain * slope


def write(built, out, chunk, sems):
    stores = []
    for tile in range(CURVES // 8):
        rows = pl.ds(pl.multiple_of(chunk * CHUNK * 8, CHUNK * 8), CHUNK * 8)
        stores.append(pltpu.make_async_copy(built.at[tile], out.at[tile, rows, :], sems.at[tile]))
        stores[-1].start()
    return stores


def rates(vol, bucket, bump):
    return [2.0 * vol[bucket[b]] + bump[b] for b in range(CURVES)]


def expand_chunks(parts, vol, bucket, bump, out, built, done):
    me = lax.axis_index("bump")
    rate = rates(vol, bucket, bump)
    stores = []
    for k, (source, turn) in enumerate(parts):
        build(source, built.at[k], rate, bucket, bump)
        stores += write(built.at[k], out, lax.rem(me + turn, WORKERS), done.at[k])
    for store in stores:
        store.wait()


def expand_kernel(own, from_m1, from_p1, vol, bucket, bump, out, built, done):
    parts = ((own, 0), (from_m1, WORKERS - 1), (from_p1, 1))
    expand_chunks(parts, vol, bucket, bump, out, built, done)


def scratch(chunks):
    tiles = CURVES // 8
    return [
        pltpu.VMEM((chunks, tiles, CHUNK * 8, LANES), jnp.float32),
        pltpu.SemaphoreType.DMA((chunks, tiles)),
    ]


def expand(own, from_m1, from_p1, vol, bucket, bump):
    return pl.pallas_call(
        expand_kernel,
        out_shape=jax.ShapeDtypeStruct((CURVES // 8, ROWS * 8, LANES), jnp.float32),
        in_specs=[vmem()] * 3 + [smem()] * 3,
        out_specs=anywhere(),
        scratch_shapes=scratch(3),
        compiler_params=params(),
        cost_estimate=EXPAND_COST,
        name="expand",
    )(own, from_m1, from_p1, vol, bucket, bump)


def complete_kernel(low, high, vol, bucket, bump, started, out, picks, joined, built, done):
    del started
    rate = rates(vol, bucket, bump)
    row = lax.broadcasted_iota(jnp.int32, (CURVES, LANES), 0)
    lane = lax.broadcasted_iota(jnp.int32, (CURVES, LANES), 1)
    pick = jnp.zeros((CURVES, LANES), jnp.float32)
    for b in range(CURVES):
        pick = jnp.where(jnp.logical_and(row == b, lane == bucket[b]), rate[b], pick)
    picks[...] = pick
    joined[0:HALF, :] = low[...]
    joined[HALF:, :] = high[...]
    expand_chunks(((joined, WORKERS - 2),), vol, bucket, bump, out, built, done)


def complete(low, high, vol, bucket, bump, started):
    tiles = CURVES // 8
    laid, picks = pl.pallas_call(
        complete_kernel,
        out_shape=(
            jax.ShapeDtypeStruct(started.shape, started.dtype),
            jax.ShapeDtypeStruct((CURVES, LANES), jnp.float32),
        ),
        in_specs=[vmem()] * 2 + [smem()] * 3 + [anywhere()],
        out_specs=(anywhere(), vmem()),
        scratch_shapes=[pltpu.VMEM((VALUES, LANES), jnp.float32)] + scratch(1),
        input_output_aliases={5: 0},
        compiler_params=params(),
        cost_estimate=EXPAND_COST,
        name="complete",
    )(low, high, vol, bucket, bump, started)
    curves = laid.reshape(tiles, ROWS, 8, LANES).transpose(0, 2, 1, 3)
    return curves.reshape(CURVES, ROWS * LANES), picks


def vega_kernel(shared, picks, vega):
    totals = jnp.sum(shared[...], axis=0, keepdims=True)
    entry = jnp.sum(picks[...] * totals, axis=1, keepdims=True)
    row = lax.broadcasted_iota(jnp.int32, (CURVES, LANES), 0)
    lane = lax.broadcasted_iota(jnp.int32, (CURVES, LANES), 1)
    line = jnp.sum(jnp.where(lane == row, entry, 0.0), axis=0, keepdims=True)
    vega[...] = line[:, :CURVES]


def vegas(shared, picks):
    return pl.pallas_call(
        vega_kernel,
        out_shape=jax.ShapeDtypeStruct((1, CURVES), jnp.float32),
        in_specs=[vmem(), vmem()],
        out_specs=vmem(),
        compiler_params=params(),
        name="vegas",
    )(shared, picks).reshape(CURVES)


def rotated(by):
    return [(i, (i + by) % WORKERS) for i in range(WORKERS)]


def on_device(payoff, positions, tables, offsets, vol_curve, bucket, bump_size):
    groups = lax.axis_size(NODE_AXES)
    with_next = [(i, i ^ 1) for i in range(groups)]
    with_last = [(i, (i + (1 if i % 2 else groups - 1)) % groups) for i in range(groups)]
    payoff_rows = payoff.reshape(ROWS, LANES)
    tables = tables.transpose(1, 0, 2).reshape(ROWS_PER_STEP, LOCAL_STEPS, ROWS, LANES)
    tables = tables.transpose(0, 2, 1, 3).reshape(ROWS_PER_STEP, PAIRS, LANES)
    to_ends = [(2 * groups + i, (i + 1) % groups) for i in range(groups)]
    to_ends += [(groups + i, 3 * groups + (i + groups - 1) % groups) for i in range(groups)]
    held, payoff_rows, position_rows, offsets, plus2, one, two, far = first(
        tables, payoff_rows, positions.reshape(ROWS, LANES), offsets
    )
    far = lax.ppermute(far, ALL_AXES, to_ends)
    from_m2 = lax.ppermute(plus2, "bump", rotated(2))
    one = lax.ppermute(one, NODE_AXES, with_next)
    two = lax.ppermute(two, NODE_AXES, with_last)
    own, plus1, plus3 = pack_near(held, one, two)
    received = (
        own,
        lax.ppermute(plus1, "bump", rotated(1)),
        from_m2,
        lax.ppermute(plus3, "bump", rotated(-1)),
    )
    peers = lax.axis_size(ALL_AXES)
    arrays, sums = roll_back(
        received, payoff_rows, position_rows, offsets, one, two, far, vol_curve, peers
    )
    from_m1 = lax.ppermute(arrays, "bump", rotated(1))
    from_p1 = lax.ppermute(arrays, "bump", rotated(-1))
    low = lax.ppermute(from_m1[:HALF], "bump", rotated(1))
    high = lax.ppermute(from_p1[HALF:], "bump", rotated(-1))
    started = expand(arrays, from_m1, from_p1, vol_curve, bucket, bump_size)
    bumped_values, picks = complete(low, high, vol_curve, bucket, bump_size, started)
    shared = lax.all_to_all(
        sums.reshape(peers, 1, LANES), ALL_AXES, split_axis=0, concat_axis=0, tiled=True
    )
    return (bumped_values, vegas(shared.reshape(peers, LANES), picks))


def solution(mesh):
    in_specs = (
        P(("nx", "ny")),
        P(("nx", "ny")),
        P("bump", None, ("nx", "ny")),
        P(None, ("nx", "ny")),
        P(),
        P("bump"),
        P("bump"),
    )
    out_specs = (P("bump", ("nx", "ny")), P("bump"))
    return jax.shard_map(
        on_device, mesh=mesh, in_specs=in_specs, out_specs=out_specs, check_vma=False
    )
```

```python
import jax
import jax.numpy as jnp
from jax import lax
from jax.experimental import pallas as pl
from jax.experimental.pallas import tpu as pltpu
from jax.sharding import PartitionSpec as P

NODE_AXES = ("nx", "ny")
ALL_AXES = ("bump", "nx", "ny")
LANES = 128
ROWS_PER_STEP = 5
STEPS = 8
WORKERS = 4
LOCAL_STEPS = STEPS // WORKERS
LOCAL_ROWS = LOCAL_STEPS * ROWS_PER_STEP
CURVES = 16
VMEM_LIMIT = 48 * 1024 * 1024

ROWS = 256
CHUNK = ROWS // WORKERS
PADDED = CHUNK + 8
PAIRS = LOCAL_STEPS * ROWS
CHUNK_PAIRS = LOCAL_STEPS * CHUNK
PADDED_PAIRS = LOCAL_STEPS * PADDED
TABLE_ROWS = LOCAL_ROWS * CHUNK
GHOST_ROWS = 24
MESSAGE = TABLE_ROWS + GHOST_ROWS
HALO = 24
VALUES = (STEPS + 1) * CHUNK
HALF = VALUES // 2

EXPAND_COST = pl.CostEstimate(flops=100_000_000, bytes_accessed=100_000_000, transcendentals=0)

VMEM = pltpu.MemorySpace.VMEM
SMEM = pltpu.MemorySpace.SMEM


def params(limit=VMEM_LIMIT):
    return pltpu.CompilerParams(vmem_limit_bytes=limit)


def vmem():
    return pl.BlockSpec(memory_space=VMEM)


def smem():
    return pl.BlockSpec(memory_space=SMEM)


def anywhere():
    return pl.BlockSpec(memory_space=pl.ANY)


def in_hbm(array):
    return pltpu.with_memory_space_constraint(array, pltpu.HBM)


def hbm():
    return pl.BlockSpec(memory_space=pltpu.HBM)


def on_even_group():
    return lax.rem(lax.axis_index("ny"), 2) == 0


def halos(one, two):
    even = on_even_group()
    return jnp.where(even, two[...], one[...]), jnp.where(even, one[...], two[...])


def pack_one(tables, k, out, before, after):
    chunk = lax.rem(lax.axis_index("bump") + k, WORKERS)
    start = pl.multiple_of(chunk * CHUNK_PAIRS, CHUNK_PAIRS)
    low = pl.multiple_of(lax.rem(start + PAIRS - 8, PAIRS), 8)
    high = pl.multiple_of(lax.rem(start + CHUNK_PAIRS, PAIRS), CHUNK_PAIRS)
    for i in range(ROWS_PER_STEP):
        out[i * CHUNK_PAIRS : (i + 1) * CHUNK_PAIRS, :] = tables[i, pl.ds(start, CHUNK_PAIRS), :]
        at = slice(i * LOCAL_STEPS, (i + 1) * LOCAL_STEPS)
        beside = tables[i, pl.ds(low, 8), :][8 - LOCAL_STEPS :]
        if before is not None:
            beside = jnp.where(chunk == 0, before[at, :], beside)
        row = TABLE_ROWS + i * LOCAL_STEPS
        out[row : row + LOCAL_STEPS, :] = beside
        beside = tables[i, pl.ds(high, 8), :][:LOCAL_STEPS]
        if after is not None:
            beside = jnp.where(chunk == WORKERS - 1, after[at, :], beside)
        row += LOCAL_ROWS
        out[row : row + LOCAL_STEPS, :] = beside
    out[TABLE_ROWS + 2 * LOCAL_ROWS :, :] = jnp.zeros(
        (GHOST_ROWS - 2 * LOCAL_ROWS, LANES), jnp.float32
    )


def first_kernel(
    tables,
    payoff,
    positions,
    offsets,
    held_tables,
    held_payoff,
    held_positions,
    held_offsets,
    plus2,
    one,
    two,
    far,
    ends,
    sem,
):
    held = (held_tables, held_payoff, held_positions, held_offsets)
    copies = [
        pltpu.make_async_copy(source, target, sem.at[i])
        for i, (source, target) in enumerate(zip((tables, payoff, positions, offsets), held))
    ]
    for copy in copies:
        copy.start()
    for copy in copies:
        copy.wait()
    pack_one(held_tables, 2, plus2, None, None)
    for side, pair, row, lane in ((0, 0, 0, 0), (1, PAIRS - LOCAL_STEPS, ROWS - 1, LANES - 1)):
        out = ends.at[side]
        for i in range(ROWS_PER_STEP):
            out[i * LOCAL_STEPS : (i + 1) * LOCAL_STEPS, :] = held_tables[
                i, pair : pair + LOCAL_STEPS, :
            ]
        out[LOCAL_ROWS : 2 * STEPS, :] = jnp.broadcast_to(
            held_payoff[row : row + 1, :], (2 * STEPS - LOCAL_ROWS, LANES)
        )
        out[2 * STEPS : HALO, :] = jnp.broadcast_to(
            held_offsets[:, lane : lane + 1].astype(jnp.float32), (STEPS, LANES)
        )
    one[...] = jnp.where(on_even_group(), ends[1], ends[0])
    two[...] = jnp.where(on_even_group(), ends[0], ends[1])
    far[...] = jnp.where(lax.axis_index("bump") == WORKERS // 2, ends[1], ends[0])


def first(*arrays):
    same = tuple(jax.ShapeDtypeStruct(array.shape, array.dtype) for array in arrays)
    message = jax.ShapeDtypeStruct((MESSAGE, LANES), jnp.float32)
    halo = jax.ShapeDtypeStruct((HALO, LANES), jnp.float32)
    return pl.pallas_call(
        first_kernel,
        out_shape=same + (message, halo, halo, halo),
        in_specs=[hbm()] * len(arrays),
        out_specs=(vmem(),) * (len(arrays) + 4),
        scratch_shapes=[
            pltpu.VMEM((2, HALO, LANES), jnp.float32),
            pltpu.SemaphoreType.DMA((len(arrays),)),
        ],
        compiler_params=params(),
        name="first",
    )(*(in_hbm(array) for array in arrays))


def pack_near_kernel(tables, one, two, own, plus1, plus3):
    before, after = halos(one, two)
    for k, out in ((1, plus1), (3, plus3), (0, own)):
        pack_one(tables, k, out, before, after)


def pack_near(tables, one, two):
    shape = jax.ShapeDtypeStruct((MESSAGE, LANES), jnp.float32)
    return pl.pallas_call(
        pack_near_kernel,
        out_shape=(shape,) * 3,
        in_specs=[vmem()] * 3,
        out_specs=(vmem(),) * 3,
        compiler_params=params(),
        name="pack",
    )(tables, one, two)


def shifted(values, by, lane):
    if by == 0:
        return values
    turned = pltpu.roll(values, (-by) % LANES, 1)
    if by > 0:
        return jnp.where(lane < LANES - by, turned, pltpu.roll(turned, PADDED - 1, 0))
    return jnp.where(lane >= -by, turned, pltpu.roll(turned, 1, 0))


def spread(low, even, down, middle, up):
    zero = jnp.zeros_like(up)
    return (
        jnp.where(low, down, zero),
        jnp.where(low, middle, jnp.where(even, down, zero)),
        jnp.where(low, up, jnp.where(even, middle, down)),
        jnp.where(low, zero, jnp.where(even, up, middle)),
        jnp.where(even, zero, up),
    )


def weigh(weights, reach):
    total = weights[0] * reach[0]
    for weight, value in zip(weights[1:], reach[1:]):
        total = total + weight * value
    return total


def prepare_kernel(payoff, offsets, one, two, out, nodes_k, steps_k):
    me = lax.axis_index("bump")
    before, after = halos(one, two)
    turned = jnp.transpose(offsets[...].astype(jnp.float32))
    steps_k[8 : 8 + ROWS, :] = jnp.repeat(turned, ROWS // LANES, axis=0)
    steps_k[0:8, :] = jnp.transpose(before[2 * STEPS : HALO, 0:8])
    steps_k[8 + ROWS :, :] = jnp.transpose(after[2 * STEPS : HALO, 0:8])
    start = pl.multiple_of(me * CHUNK, CHUNK)
    part = jnp.concatenate(
        [
            steps_k[pl.ds(start + 8, CHUNK + 1), :],
            jnp.zeros((PADDED - CHUNK - 2, STEPS), jnp.float32),
            steps_k[pl.ds(start + 7, 1), :],
        ]
    )
    for s in range(STEPS):
        nodes_k[s] = jnp.broadcast_to(part[:, s : s + 1], (PADDED, LANES))
    above = payoff[pl.ds(pl.multiple_of(jnp.minimum(start + CHUNK, ROWS - 8), 8), 8), :]
    below = payoff[pl.ds(pl.multiple_of(jnp.maximum(start - 8, 0), 8), 8), :]
    out[...] = jnp.concatenate(
        [
            payoff[pl.ds(start, CHUNK), :],
            jnp.where(me == WORKERS - 1, after[LOCAL_ROWS : LOCAL_ROWS + 1, :], above[0:1, :]),
            jnp.zeros((PADDED - CHUNK - 2, LANES), jnp.float32),
            jnp.where(me == 0, before[LOCAL_ROWS : LOCAL_ROWS + 1, :], below[7:8, :]),
        ]
    )


def prepare(payoff, offsets, one, two):
    return pl.pallas_call(
        prepare_kernel,
        out_shape=(
            jax.ShapeDtypeStruct((PADDED, LANES), jnp.float32),
            jax.ShapeDtypeStruct((STEPS, PADDED, LANES), jnp.float32),
        ),
        in_specs=[vmem()] * 4,
        out_specs=(vmem(), vmem()),
        scratch_shapes=[pltpu.VMEM((ROWS + 16, STEPS), jnp.float32)],
        compiler_params=params(),
        name="prepare",
    )(payoff, offsets, one, two)


def roll_kernel(
    own,
    from_m1,
    from_m2,
    from_p1,
    payoff,
    nodes_k,
    positions,
    far,
    vol,
    out,
    sums,
    table,
):
    me = lax.axis_index("bump")
    sources = (own, from_m1, from_m2, from_p1)
    turns = (0, WORKERS - 1, WORKERS - 2, 1)
    start = pl.multiple_of(me * CHUNK, CHUNK)
    gap = jnp.zeros((PADDED_PAIRS - CHUNK_PAIRS - 2 * LOCAL_STEPS, LANES), jnp.float32)
    for k in range(WORKERS):
        owner = lax.rem(me + turns[k], WORKERS)
        source = sources[k]
        for i in range(ROWS_PER_STEP):
            table[owner, i, :CHUNK_PAIRS, :] = source[i * CHUNK_PAIRS : (i + 1) * CHUNK_PAIRS, :]
            at = slice(i * LOCAL_STEPS, (i + 1) * LOCAL_STEPS)
            low = TABLE_ROWS + i * LOCAL_STEPS
            high = low + LOCAL_ROWS
            ahead = source[low : low + LOCAL_STEPS, :]
            behind = source[high : high + LOCAL_STEPS, :]
            if k == 2:
                ahead = jnp.where(me == 0, far[at, :], ahead)
                behind = jnp.where(me == WORKERS - 1, far[at, :], behind)
            table[owner, i, CHUNK_PAIRS:, :] = jnp.concatenate([behind, gap, ahead])

    def rows(s, i):
        return table[s // LOCAL_STEPS, i, pl.ds(s % LOCAL_STEPS, PADDED, stride=LOCAL_STEPS), :]

    lane = lax.broadcasted_iota(jnp.int32, (PADDED, LANES), 1)
    values = payoff[...]
    slopes = {}
    for s in reversed(range(STEPS)):
        variance = vol[s] * vol[s]
        discount = rows(s, 0)
        up_slope = discount * rows(s, 2)
        down_slope = discount * rows(s, 4)
        up = discount * rows(s, 1) + variance * up_slope
        down = discount * rows(s, 3) + variance * down_slope
        low, even = nodes_k[s] < -0.5, nodes_k[s] < 0.5
        weights = spread(low, even, down, discount - up - down, up)
        slope_weights = spread(low, even, down_slope, -(up_slope + down_slope), up_slope)
        for q in list(slopes):
            reach = [shifted(slopes[q], m, lane) for m in range(-2, 3)]
            slopes[q] = weigh(weights, reach)
        reach = [shifted(values, m, lane) for m in range(-2, 3)]
        slopes[s] = weigh(slope_weights, reach)
        values = weigh(weights, reach)
    out[0:CHUNK, :] = values[0:CHUNK]
    weight = positions[pl.ds(start, CHUNK), :]
    lines = []
    for s in range(STEPS):
        slope = slopes[s][0:CHUNK]
        out[(s + 1) * CHUNK : (s + 2) * CHUNK, :] = slope
        lines.append(jnp.sum(weight * slope, axis=0, keepdims=True))
    totals = jnp.sum(jnp.concatenate(lines), axis=1, keepdims=True)
    step = lax.broadcasted_iota(jnp.int32, (STEPS, LANES), 0)
    own_lane = lax.broadcasted_iota(jnp.int32, (STEPS, LANES), 1) == step
    line = jnp.sum(jnp.where(own_lane, totals, 0.0), axis=0, keepdims=True)
    sums[...] = jnp.broadcast_to(line, sums.shape)


def roll_back(messages, payoff, nodes_k, positions, far, vol, peers):
    return pl.pallas_call(
        roll_kernel,
        out_shape=(
            jax.ShapeDtypeStruct((VALUES, LANES), jnp.float32),
            jax.ShapeDtypeStruct((peers, LANES), jnp.float32),
        ),
        in_specs=[vmem()] * (WORKERS + 4) + [smem()],
        out_specs=(vmem(), vmem()),
        scratch_shapes=[
            pltpu.VMEM((WORKERS, ROWS_PER_STEP, PADDED_PAIRS, LANES), jnp.float32),
        ],
        compiler_params=params(),
        name="roll_back",
    )(*messages, payoff, nodes_k, positions, far, vol)


def build(source, built, out, chunk, rate, bucket, bump, sems):
    base = source[0:CHUNK, :]
    rows = pl.ds(pl.multiple_of(chunk * CHUNK * 8, CHUNK * 8), CHUNK * 8)
    stores = []
    for tile in range(CURVES // 8):
        for r in range(8):
            b = tile * 8 + r
            gain = bump[b] * rate[b]
            slope = source[pl.ds(pl.multiple_of((bucket[b] + 1) * CHUNK, CHUNK), CHUNK), :]
            built[tile, pl.ds(r, CHUNK, stride=8), :] = base + gain * slope
        stores.append(pltpu.make_async_copy(built.at[tile], out.at[tile, rows, :], sems.at[tile]))
        stores[-1].start()
    return stores


def rates(vol, bucket, bump):
    return [2.0 * vol[bucket[b]] + bump[b] for b in range(CURVES)]


def expand_chunks(parts, vol, bucket, bump, out, built, done):
    me = lax.axis_index("bump")
    rate = rates(vol, bucket, bump)
    stores = []
    for k, (source, turn) in enumerate(parts):
        chunk = lax.rem(me + turn, WORKERS)
        stores += build(source, built.at[k], out, chunk, rate, bucket, bump, done.at[k])
    for store in stores:
        store.wait()


def expand_kernel(own, from_m1, from_p1, vol, bucket, bump, out, built, done):
    parts = ((own, 0), (from_m1, WORKERS - 1), (from_p1, 1))
    expand_chunks(parts, vol, bucket, bump, out, built, done)


def scratch(chunks):
    tiles = CURVES // 8
    return [
        pltpu.VMEM((chunks, tiles, CHUNK * 8, LANES), jnp.float32),
        pltpu.SemaphoreType.DMA((chunks, tiles)),
    ]


def expand(own, from_m1, from_p1, vol, bucket, bump):
    return pl.pallas_call(
        expand_kernel,
        out_shape=jax.ShapeDtypeStruct((CURVES // 8, ROWS * 8, LANES), jnp.float32),
        in_specs=[vmem()] * 3 + [smem()] * 3,
        out_specs=anywhere(),
        scratch_shapes=scratch(3),
        compiler_params=params(),
        cost_estimate=EXPAND_COST,
        name="expand",
    )(own, from_m1, from_p1, vol, bucket, bump)


def complete_kernel(low, high, vol, bucket, bump, started, out, picks, joined, built, done):
    del started
    rate = rates(vol, bucket, bump)
    row = lax.broadcasted_iota(jnp.int32, (CURVES, LANES), 0)
    lane = lax.broadcasted_iota(jnp.int32, (CURVES, LANES), 1)
    pick = jnp.zeros((CURVES, LANES), jnp.float32)
    for b in range(CURVES):
        pick = jnp.where(jnp.logical_and(row == b, lane == bucket[b]), rate[b], pick)
    picks[...] = pick
    joined[0:HALF, :] = low[...]
    joined[HALF:, :] = high[...]
    expand_chunks(((joined, WORKERS - 2),), vol, bucket, bump, out, built, done)


def complete(low, high, vol, bucket, bump, started):
    tiles = CURVES // 8
    laid, picks = pl.pallas_call(
        complete_kernel,
        out_shape=(
            jax.ShapeDtypeStruct(started.shape, started.dtype),
            jax.ShapeDtypeStruct((CURVES, LANES), jnp.float32),
        ),
        in_specs=[vmem()] * 2 + [smem()] * 3 + [anywhere()],
        out_specs=(anywhere(), vmem()),
        scratch_shapes=[pltpu.VMEM((VALUES, LANES), jnp.float32)] + scratch(1),
        input_output_aliases={5: 0},
        compiler_params=params(),
        cost_estimate=EXPAND_COST,
        name="complete",
    )(low, high, vol, bucket, bump, started)
    curves = laid.reshape(tiles, ROWS, 8, LANES).transpose(0, 2, 1, 3)
    return curves.reshape(CURVES, ROWS * LANES), picks


def vega_kernel(shared, picks, vega):
    totals = jnp.sum(shared[...], axis=0, keepdims=True)
    entry = jnp.sum(picks[...] * totals, axis=1, keepdims=True)
    row = lax.broadcasted_iota(jnp.int32, (CURVES, LANES), 0)
    lane = lax.broadcasted_iota(jnp.int32, (CURVES, LANES), 1)
    line = jnp.sum(jnp.where(lane == row, entry, 0.0), axis=0, keepdims=True)
    vega[...] = line[:, :CURVES]


def vegas(shared, picks):
    return pl.pallas_call(
        vega_kernel,
        out_shape=jax.ShapeDtypeStruct((1, CURVES), jnp.float32),
        in_specs=[vmem(), vmem()],
        out_specs=vmem(),
        compiler_params=params(),
        name="vegas",
    )(shared, picks).reshape(CURVES)


def rotated(by):
    return [(i, (i + by) % WORKERS) for i in range(WORKERS)]


def on_device(payoff, positions, tables, offsets, vol_curve, bucket, bump_size):
    groups = lax.axis_size(NODE_AXES)
    with_next = [(i, i ^ 1) for i in range(groups)]
    with_last = [(i, (i + (1 if i % 2 else groups - 1)) % groups) for i in range(groups)]
    payoff_rows = payoff.reshape(ROWS, LANES)
    tables = tables.transpose(1, 0, 2).reshape(ROWS_PER_STEP, LOCAL_STEPS, ROWS, LANES)
    tables = tables.transpose(0, 2, 1, 3).reshape(ROWS_PER_STEP, PAIRS, LANES)
    to_ends = [(2 * groups + i, (i + 1) % groups) for i in range(groups)]
    to_ends += [(groups + i, 3 * groups + (i + groups - 1) % groups) for i in range(groups)]
    held, payoff_rows, position_rows, offsets, plus2, one, two, far = first(
        tables, payoff_rows, positions.reshape(ROWS, LANES), offsets
    )
    far = lax.ppermute(far, ALL_AXES, to_ends)
    from_m2 = lax.ppermute(plus2, "bump", rotated(2))
    one = lax.ppermute(one, NODE_AXES, with_next)
    two = lax.ppermute(two, NODE_AXES, with_last)
    own, plus1, plus3 = pack_near(held, one, two)
    received = (
        own,
        lax.ppermute(plus1, "bump", rotated(1)),
        from_m2,
        lax.ppermute(plus3, "bump", rotated(-1)),
    )
    peers = lax.axis_size(ALL_AXES)
    payoff_part, nodes_k = prepare(payoff_rows, offsets, one, two)
    arrays, sums = roll_back(
        received, payoff_part, nodes_k, position_rows, far, vol_curve, peers
    )
    from_m1 = lax.ppermute(arrays, "bump", rotated(1))
    from_p1 = lax.ppermute(arrays, "bump", rotated(-1))
    low = lax.ppermute(from_m1[:HALF], "bump", rotated(1))
    high = lax.ppermute(from_p1[HALF:], "bump", rotated(-1))
    started = expand(arrays, from_m1, from_p1, vol_curve, bucket, bump_size)
    bumped_values, picks = complete(low, high, vol_curve, bucket, bump_size, started)
    shared = lax.all_to_all(
        sums.reshape(peers, 1, LANES), ALL_AXES, split_axis=0, concat_axis=0, tiled=True
    )
    return (bumped_values, vegas(shared.reshape(peers, LANES), picks))


def solution(mesh):
    in_specs = (
        P(("nx", "ny")),
        P(("nx", "ny")),
        P("bump", None, ("nx", "ny")),
        P(None, ("nx", "ny")),
        P(),
        P("bump"),
        P("bump"),
    )
    out_specs = (P("bump", ("nx", "ny")), P("bump"))
    return jax.shard_map(
        on_device, mesh=mesh, in_specs=in_specs, out_specs=out_specs, check_vma=False
    )
```

```python
import jax
import jax.numpy as jnp
from jax import lax
from jax.experimental import pallas as pl
from jax.experimental.pallas import tpu as pltpu
from jax.sharding import PartitionSpec as P

NODE_AXES = ("nx", "ny")
ALL_AXES = ("bump", "nx", "ny")
LANES = 128
ROWS_PER_STEP = 5
STEPS = 8
WORKERS = 4
LOCAL_STEPS = STEPS // WORKERS
LOCAL_ROWS = LOCAL_STEPS * ROWS_PER_STEP
CURVES = 16
VMEM_LIMIT = 48 * 1024 * 1024

ROWS = 256
CHUNK = ROWS // WORKERS
PADDED = CHUNK + 8
PAIRS = LOCAL_STEPS * ROWS
CHUNK_PAIRS = LOCAL_STEPS * CHUNK
PADDED_PAIRS = LOCAL_STEPS * PADDED
TABLE_ROWS = LOCAL_ROWS * CHUNK
GHOST_ROWS = 24
MESSAGE = TABLE_ROWS + GHOST_ROWS
HALO = 24
VALUES = (STEPS + 1) * CHUNK
HALF = VALUES // 2

EXPAND_COST = pl.CostEstimate(flops=100_000_000, bytes_accessed=100_000_000, transcendentals=0)

VMEM = pltpu.MemorySpace.VMEM
SMEM = pltpu.MemorySpace.SMEM


def params(limit=VMEM_LIMIT):
    return pltpu.CompilerParams(vmem_limit_bytes=limit)


def vmem():
    return pl.BlockSpec(memory_space=VMEM)


def smem():
    return pl.BlockSpec(memory_space=SMEM)


def anywhere():
    return pl.BlockSpec(memory_space=pl.ANY)


def in_hbm(array):
    return pltpu.with_memory_space_constraint(array, pltpu.HBM)


def hbm():
    return pl.BlockSpec(memory_space=pltpu.HBM)


def on_even_group():
    return lax.rem(lax.axis_index("ny"), 2) == 0


def halos(one, two):
    even = on_even_group()
    return jnp.where(even, two[...], one[...]), jnp.where(even, one[...], two[...])


def pack_one(tables, k, out, before, after):
    chunk = lax.rem(lax.axis_index("bump") + k, WORKERS)
    start = pl.multiple_of(chunk * CHUNK_PAIRS, CHUNK_PAIRS)
    low = pl.multiple_of(lax.rem(start + PAIRS - 8, PAIRS), 8)
    high = pl.multiple_of(lax.rem(start + CHUNK_PAIRS, PAIRS), CHUNK_PAIRS)
    for i in range(ROWS_PER_STEP):
        out[i * CHUNK_PAIRS : (i + 1) * CHUNK_PAIRS, :] = tables[i, pl.ds(start, CHUNK_PAIRS), :]
        at = slice(i * LOCAL_STEPS, (i + 1) * LOCAL_STEPS)
        beside = tables[i, pl.ds(low, 8), :][8 - LOCAL_STEPS :]
        if before is not None:
            beside = jnp.where(chunk == 0, before[at, :], beside)
        row = TABLE_ROWS + i * LOCAL_STEPS
        out[row : row + LOCAL_STEPS, :] = beside
        beside = tables[i, pl.ds(high, 8), :][:LOCAL_STEPS]
        if after is not None:
            beside = jnp.where(chunk == WORKERS - 1, after[at, :], beside)
        row += LOCAL_ROWS
        out[row : row + LOCAL_STEPS, :] = beside
    out[TABLE_ROWS + 2 * LOCAL_ROWS :, :] = jnp.zeros(
        (GHOST_ROWS - 2 * LOCAL_ROWS, LANES), jnp.float32
    )


def first_kernel(
    tables,
    payoff,
    positions,
    offsets,
    held_tables,
    held_payoff,
    held_positions,
    held_offsets,
    plus2,
    one,
    two,
    far,
    ends,
    sem,
):
    held = (held_tables, held_payoff, held_positions, held_offsets)
    copies = [
        pltpu.make_async_copy(source, target, sem.at[i])
        for i, (source, target) in enumerate(zip((tables, payoff, positions, offsets), held))
    ]
    for copy in copies:
        copy.start()
    for copy in copies:
        copy.wait()
    pack_one(held_tables, 2, plus2, None, None)
    for side, pair, row, lane in ((0, 0, 0, 0), (1, PAIRS - LOCAL_STEPS, ROWS - 1, LANES - 1)):
        out = ends.at[side]
        for i in range(ROWS_PER_STEP):
            out[i * LOCAL_STEPS : (i + 1) * LOCAL_STEPS, :] = held_tables[
                i, pair : pair + LOCAL_STEPS, :
            ]
        out[LOCAL_ROWS : 2 * STEPS, :] = jnp.broadcast_to(
            held_payoff[row : row + 1, :], (2 * STEPS - LOCAL_ROWS, LANES)
        )
        out[2 * STEPS : HALO, :] = jnp.broadcast_to(
            held_offsets[:, lane : lane + 1].astype(jnp.float32), (STEPS, LANES)
        )
    one[...] = jnp.where(on_even_group(), ends[1], ends[0])
    two[...] = jnp.where(on_even_group(), ends[0], ends[1])
    far[...] = jnp.where(lax.axis_index("bump") == WORKERS // 2, ends[1], ends[0])


def first(*arrays):
    same = tuple(jax.ShapeDtypeStruct(array.shape, array.dtype) for array in arrays)
    message = jax.ShapeDtypeStruct((MESSAGE, LANES), jnp.float32)
    halo = jax.ShapeDtypeStruct((HALO, LANES), jnp.float32)
    return pl.pallas_call(
        first_kernel,
        out_shape=same + (message, halo, halo, halo),
        in_specs=[hbm()] * len(arrays),
        out_specs=(vmem(),) * (len(arrays) + 4),
        scratch_shapes=[
            pltpu.VMEM((2, HALO, LANES), jnp.float32),
            pltpu.SemaphoreType.DMA((len(arrays),)),
        ],
        compiler_params=params(),
        name="first",
    )(*(in_hbm(array) for array in arrays))


def pack_near_kernel(tables, one, two, own, plus1, plus3):
    before, after = halos(one, two)
    for k, out in ((1, plus1), (3, plus3), (0, own)):
        pack_one(tables, k, out, before, after)


def pack_near(tables, one, two):
    shape = jax.ShapeDtypeStruct((MESSAGE, LANES), jnp.float32)
    return pl.pallas_call(
        pack_near_kernel,
        out_shape=(shape,) * 3,
        in_specs=[vmem()] * 3,
        out_specs=(vmem(),) * 3,
        compiler_params=params(),
        name="pack",
    )(tables, one, two)


def shifted(values, by, lane):
    if by == 0:
        return values
    turned = pltpu.roll(values, (-by) % LANES, 1)
    if by > 0:
        return jnp.where(lane < LANES - by, turned, pltpu.roll(turned, PADDED - 1, 0))
    return jnp.where(lane >= -by, turned, pltpu.roll(turned, 1, 0))


def spread(low, even, down, middle, up):
    zero = jnp.zeros_like(up)
    return (
        jnp.where(low, down, zero),
        jnp.where(low, middle, jnp.where(even, down, zero)),
        jnp.where(low, up, jnp.where(even, middle, down)),
        jnp.where(low, zero, jnp.where(even, up, middle)),
        jnp.where(even, zero, up),
    )


def weigh(weights, reach):
    total = weights[0] * reach[0]
    for weight, value in zip(weights[1:], reach[1:]):
        total = total + weight * value
    return total


def roll_kernel(
    own,
    from_m1,
    from_m2,
    from_p1,
    payoff,
    positions,
    offsets,
    one,
    two,
    far,
    vol,
    out,
    sums,
    table,
    steps_k,
    nodes_k,
):
    me = lax.axis_index("bump")
    before, after = halos(one, two)
    sources = (own, from_m1, from_m2, from_p1)
    turns = (0, WORKERS - 1, WORKERS - 2, 1)
    turned = jnp.transpose(offsets[...].astype(jnp.float32))
    steps_k[8 : 8 + ROWS, :] = jnp.repeat(turned, ROWS // LANES, axis=0)
    steps_k[0:8, :] = jnp.transpose(before[2 * STEPS : HALO, 0:8])
    steps_k[8 + ROWS :, :] = jnp.transpose(after[2 * STEPS : HALO, 0:8])
    start = pl.multiple_of(me * CHUNK, CHUNK)
    part = jnp.concatenate(
        [
            steps_k[pl.ds(start + 8, CHUNK + 1), :],
            jnp.zeros((PADDED - CHUNK - 2, STEPS), jnp.float32),
            steps_k[pl.ds(start + 7, 1), :],
        ]
    )
    for s in range(STEPS):
        nodes_k[s] = jnp.broadcast_to(part[:, s : s + 1], (PADDED, LANES))
    above = payoff[pl.ds(pl.multiple_of(jnp.minimum(start + CHUNK, ROWS - 8), 8), 8), :]
    below = payoff[pl.ds(pl.multiple_of(jnp.maximum(start - 8, 0), 8), 8), :]
    values = jnp.concatenate(
        [
            payoff[pl.ds(start, CHUNK), :],
            jnp.where(me == WORKERS - 1, after[LOCAL_ROWS : LOCAL_ROWS + 1, :], above[0:1, :]),
            jnp.zeros((PADDED - CHUNK - 2, LANES), jnp.float32),
            jnp.where(me == 0, before[LOCAL_ROWS : LOCAL_ROWS + 1, :], below[7:8, :]),
        ]
    )
    gap = jnp.zeros((PADDED_PAIRS - CHUNK_PAIRS - 2 * LOCAL_STEPS, LANES), jnp.float32)
    for k in range(WORKERS):
        owner = lax.rem(me + turns[k], WORKERS)
        source = sources[k]
        for i in range(ROWS_PER_STEP):
            table[owner, i, :CHUNK_PAIRS, :] = source[i * CHUNK_PAIRS : (i + 1) * CHUNK_PAIRS, :]
            at = slice(i * LOCAL_STEPS, (i + 1) * LOCAL_STEPS)
            low = TABLE_ROWS + i * LOCAL_STEPS
            high = low + LOCAL_ROWS
            ahead = source[low : low + LOCAL_STEPS, :]
            behind = source[high : high + LOCAL_STEPS, :]
            if k == 2:
                ahead = jnp.where(me == 0, far[at, :], ahead)
                behind = jnp.where(me == WORKERS - 1, far[at, :], behind)
            table[owner, i, CHUNK_PAIRS:, :] = jnp.concatenate([behind, gap, ahead])

    def rows(s, i):
        return table[s // LOCAL_STEPS, i, pl.ds(s % LOCAL_STEPS, PADDED, stride=LOCAL_STEPS), :]

    lane = lax.broadcasted_iota(jnp.int32, (PADDED, LANES), 1)
    slopes = {}
    for s in reversed(range(STEPS)):
        variance = vol[s] * vol[s]
        discount = rows(s, 0)
        up_slope = discount * rows(s, 2)
        down_slope = discount * rows(s, 4)
        up = discount * rows(s, 1) + variance * up_slope
        down = discount * rows(s, 3) + variance * down_slope
        low, even = nodes_k[s] < -0.5, nodes_k[s] < 0.5
        weights = spread(low, even, down, discount - up - down, up)
        slope_weights = spread(low, even, down_slope, -(up_slope + down_slope), up_slope)
        for q in list(slopes):
            reach = [shifted(slopes[q], m, lane) for m in range(-2, 3)]
            slopes[q] = weigh(weights, reach)
        reach = [shifted(values, m, lane) for m in range(-2, 3)]
        slopes[s] = weigh(slope_weights, reach)
        values = weigh(weights, reach)
    out[0:CHUNK, :] = values[0:CHUNK]
    weight = positions[pl.ds(start, CHUNK), :]
    lines = []
    for s in range(STEPS):
        slope = slopes[s][0:CHUNK]
        out[(s + 1) * CHUNK : (s + 2) * CHUNK, :] = slope
        lines.append(jnp.sum(weight * slope, axis=0, keepdims=True))
    totals = jnp.sum(jnp.concatenate(lines), axis=1, keepdims=True)
    step = lax.broadcasted_iota(jnp.int32, (STEPS, LANES), 0)
    own_lane = lax.broadcasted_iota(jnp.int32, (STEPS, LANES), 1) == step
    line = jnp.sum(jnp.where(own_lane, totals, 0.0), axis=0, keepdims=True)
    sums[...] = jnp.broadcast_to(line, sums.shape)


def roll_back(messages, payoff, positions, offsets, one, two, far, vol, peers):
    return pl.pallas_call(
        roll_kernel,
        out_shape=(
            jax.ShapeDtypeStruct((VALUES, LANES), jnp.float32),
            jax.ShapeDtypeStruct((peers, LANES), jnp.float32),
        ),
        in_specs=[vmem()] * (WORKERS + 6) + [smem()],
        out_specs=(vmem(), vmem()),
        scratch_shapes=[
            pltpu.VMEM((WORKERS, ROWS_PER_STEP, PADDED_PAIRS, LANES), jnp.float32),
            pltpu.VMEM((ROWS + 16, STEPS), jnp.float32),
            pltpu.VMEM((STEPS, PADDED, LANES), jnp.float32),
        ],
        compiler_params=params(),
        name="roll_back",
    )(*messages, payoff, positions, offsets, one, two, far, vol)


def build(source, tile_rows, rate, bucket, bump):
    base = source[0:CHUNK, :]
    for b in range(CURVES):
        gain = bump[b] * rate[b]
        slope = source[pl.ds(pl.multiple_of((bucket[b] + 1) * CHUNK, CHUNK), CHUNK), :]
        tile_rows[b // 8, pl.ds(b % 8, CHUNK, stride=8), :] = base + gain * slope


def write(built, out, chunk, sems):
    stores = []
    for tile in range(CURVES // 8):
        rows = pl.ds(pl.multiple_of(chunk * CHUNK * 8, CHUNK * 8), CHUNK * 8)
        stores.append(pltpu.make_async_copy(built.at[tile], out.at[tile, rows, :], sems.at[tile]))
        stores[-1].start()
    return stores


def rates(vol, bucket, bump):
    return [2.0 * vol[bucket[b]] + bump[b] for b in range(CURVES)]


def expand_chunks(parts, vol, bucket, bump, out, built, done):
    me = lax.axis_index("bump")
    rate = rates(vol, bucket, bump)
    stores = []
    for k, (source, flip) in enumerate(parts):
        build(source, built.at[k], rate, bucket, bump)
        stores += write(built.at[k], out, lax.bitwise_xor(me, flip), done.at[k])
    for store in stores:
        store.wait()


def expand_kernel(own, from_1, from_3, vol, bucket, bump, out, built, done):
    parts = ((own, 0), (from_1, 1), (from_3, 3))
    expand_chunks(parts, vol, bucket, bump, out, built, done)


def scratch(chunks):
    tiles = CURVES // 8
    return [
        pltpu.VMEM((chunks, tiles, CHUNK * 8, LANES), jnp.float32),
        pltpu.SemaphoreType.DMA((chunks, tiles)),
    ]


def expand(own, from_1, from_3, vol, bucket, bump):
    return pl.pallas_call(
        expand_kernel,
        out_shape=jax.ShapeDtypeStruct((CURVES // 8, ROWS * 8, LANES), jnp.float32),
        in_specs=[vmem()] * 3 + [smem()] * 3,
        out_specs=anywhere(),
        scratch_shapes=scratch(3),
        compiler_params=params(),
        cost_estimate=EXPAND_COST,
        name="expand",
    )(own, from_1, from_3, vol, bucket, bump)


def complete_kernel(low, high, vol, bucket, bump, started, out, picks, joined, built, done):
    del started
    rate = rates(vol, bucket, bump)
    row = lax.broadcasted_iota(jnp.int32, (CURVES, LANES), 0)
    lane = lax.broadcasted_iota(jnp.int32, (CURVES, LANES), 1)
    pick = jnp.zeros((CURVES, LANES), jnp.float32)
    for b in range(CURVES):
        pick = jnp.where(jnp.logical_and(row == b, lane == bucket[b]), rate[b], pick)
    picks[...] = pick
    joined[0:HALF, :] = low[...]
    joined[HALF:, :] = high[...]
    expand_chunks(((joined, 2),), vol, bucket, bump, out, built, done)


def complete(low, high, vol, bucket, bump, started):
    tiles = CURVES // 8
    laid, picks = pl.pallas_call(
        complete_kernel,
        out_shape=(
            jax.ShapeDtypeStruct(started.shape, started.dtype),
            jax.ShapeDtypeStruct((CURVES, LANES), jnp.float32),
        ),
        in_specs=[vmem()] * 2 + [smem()] * 3 + [anywhere()],
        out_specs=(anywhere(), vmem()),
        scratch_shapes=[pltpu.VMEM((VALUES, LANES), jnp.float32)] + scratch(1),
        input_output_aliases={5: 0},
        compiler_params=params(),
        cost_estimate=EXPAND_COST,
        name="complete",
    )(low, high, vol, bucket, bump, started)
    curves = laid.reshape(tiles, ROWS, 8, LANES).transpose(0, 2, 1, 3)
    return curves.reshape(CURVES, ROWS * LANES), picks


def vega_kernel(shared, picks, vega):
    totals = jnp.sum(shared[...], axis=0, keepdims=True)
    entry = jnp.sum(picks[...] * totals, axis=1, keepdims=True)
    row = lax.broadcasted_iota(jnp.int32, (CURVES, LANES), 0)
    lane = lax.broadcasted_iota(jnp.int32, (CURVES, LANES), 1)
    line = jnp.sum(jnp.where(lane == row, entry, 0.0), axis=0, keepdims=True)
    vega[...] = line[:, :CURVES]


def vegas(shared, picks):
    return pl.pallas_call(
        vega_kernel,
        out_shape=jax.ShapeDtypeStruct((1, CURVES), jnp.float32),
        in_specs=[vmem(), vmem()],
        out_specs=vmem(),
        compiler_params=params(),
        name="vegas",
    )(shared, picks).reshape(CURVES)


def rotated(by):
    return [(i, (i + by) % WORKERS) for i in range(WORKERS)]


def on_device(payoff, positions, tables, offsets, vol_curve, bucket, bump_size):
    groups = lax.axis_size(NODE_AXES)
    with_next = [(i, i ^ 1) for i in range(groups)]
    with_last = [(i, (i + (1 if i % 2 else groups - 1)) % groups) for i in range(groups)]
    payoff_rows = payoff.reshape(ROWS, LANES)
    tables = tables.transpose(1, 0, 2).reshape(ROWS_PER_STEP, LOCAL_STEPS, ROWS, LANES)
    tables = tables.transpose(0, 2, 1, 3).reshape(ROWS_PER_STEP, PAIRS, LANES)
    to_ends = [(2 * groups + i, (i + 1) % groups) for i in range(groups)]
    to_ends += [(groups + i, 3 * groups + (i + groups - 1) % groups) for i in range(groups)]
    held, payoff_rows, position_rows, offsets, plus2, one, two, far = first(
        tables, payoff_rows, positions.reshape(ROWS, LANES), offsets
    )
    far = lax.ppermute(far, ALL_AXES, to_ends)
    from_m2 = lax.ppermute(plus2, "bump", rotated(2))
    one = lax.ppermute(one, NODE_AXES, with_next)
    two = lax.ppermute(two, NODE_AXES, with_last)
    own, plus1, plus3 = pack_near(held, one, two)
    received = (
        own,
        lax.ppermute(plus1, "bump", rotated(1)),
        from_m2,
        lax.ppermute(plus3, "bump", rotated(-1)),
    )
    peers = lax.axis_size(ALL_AXES)
    arrays, sums = roll_back(
        received, payoff_rows, position_rows, offsets, one, two, far, vol_curve, peers
    )
    pairs = {flip: [(i, i ^ flip) for i in range(WORKERS)] for flip in (1, 3)}
    from_1 = lax.ppermute(arrays, "bump", pairs[1])
    from_3 = lax.ppermute(arrays, "bump", pairs[3])
    low = lax.ppermute(from_3[:HALF], "bump", pairs[1])
    high = lax.ppermute(from_1[HALF:], "bump", pairs[3])
    started = expand(arrays, from_1, from_3, vol_curve, bucket, bump_size)
    bumped_values, picks = complete(low, high, vol_curve, bucket, bump_size, started)
    shared = lax.all_to_all(
        sums.reshape(peers, 1, LANES), ALL_AXES, split_axis=0, concat_axis=0, tiled=True
    )
    return (bumped_values, vegas(shared.reshape(peers, LANES), picks))


def solution(mesh):
    in_specs = (
        P(("nx", "ny")),
        P(("nx", "ny")),
        P("bump", None, ("nx", "ny")),
        P(None, ("nx", "ny")),
        P(),
        P("bump"),
        P("bump"),
    )
    out_specs = (P("bump", ("nx", "ny")), P("bump"))
    return jax.shard_map(
        on_device, mesh=mesh, in_specs=in_specs, out_specs=out_specs, check_vma=False
    )
```

```python
import jax
import jax.numpy as jnp
from jax import lax
from jax.experimental import pallas as pl
from jax.experimental.pallas import tpu as pltpu
from jax.sharding import PartitionSpec as P

NODE_AXES = ("nx", "ny")
ALL_AXES = ("bump", "nx", "ny")
LANES = 128
ROWS_PER_STEP = 5
STEPS = 8
WORKERS = 4
LOCAL_STEPS = STEPS // WORKERS
LOCAL_ROWS = LOCAL_STEPS * ROWS_PER_STEP
CURVES = 16
VMEM_LIMIT = 48 * 1024 * 1024

ROWS = 256
CHUNK = ROWS // WORKERS
PADDED = CHUNK + 8
PAIRS = LOCAL_STEPS * ROWS
CHUNK_PAIRS = LOCAL_STEPS * CHUNK
PADDED_PAIRS = LOCAL_STEPS * PADDED
TABLE_ROWS = LOCAL_ROWS * CHUNK
GHOST_ROWS = 24
MESSAGE = TABLE_ROWS + GHOST_ROWS
HALO = 24
VALUES = (STEPS + 1) * CHUNK
HALF = VALUES // 2

EXPAND_COST = pl.CostEstimate(flops=100_000_000, bytes_accessed=100_000_000, transcendentals=0)

VMEM = pltpu.MemorySpace.VMEM
SMEM = pltpu.MemorySpace.SMEM


def params(limit=VMEM_LIMIT):
    return pltpu.CompilerParams(vmem_limit_bytes=limit)


def vmem():
    return pl.BlockSpec(memory_space=VMEM)


def smem():
    return pl.BlockSpec(memory_space=SMEM)


def anywhere():
    return pl.BlockSpec(memory_space=pl.ANY)


def in_hbm(array):
    return pltpu.with_memory_space_constraint(array, pltpu.HBM)


def hbm():
    return pl.BlockSpec(memory_space=pltpu.HBM)


def on_even_group():
    return lax.rem(lax.axis_index("ny"), 2) == 0


def halos(one, two):
    even = on_even_group()
    return jnp.where(even, two[...], one[...]), jnp.where(even, one[...], two[...])


def pack_one(tables, k, out, before, after):
    chunk = lax.bitwise_xor(lax.axis_index("bump"), k)
    start = pl.multiple_of(chunk * CHUNK_PAIRS, CHUNK_PAIRS)
    low = pl.multiple_of(lax.rem(start + PAIRS - 8, PAIRS), 8)
    high = pl.multiple_of(lax.rem(start + CHUNK_PAIRS, PAIRS), CHUNK_PAIRS)
    for i in range(ROWS_PER_STEP):
        out[i * CHUNK_PAIRS : (i + 1) * CHUNK_PAIRS, :] = tables[i, pl.ds(start, CHUNK_PAIRS), :]
        at = slice(i * LOCAL_STEPS, (i + 1) * LOCAL_STEPS)
        beside = tables[i, pl.ds(low, 8), :][8 - LOCAL_STEPS :]
        if before is not None:
            beside = jnp.where(chunk == 0, before[at, :], beside)
        row = TABLE_ROWS + i * LOCAL_STEPS
        out[row : row + LOCAL_STEPS, :] = beside
        beside = tables[i, pl.ds(high, 8), :][:LOCAL_STEPS]
        if after is not None:
            beside = jnp.where(chunk == WORKERS - 1, after[at, :], beside)
        row += LOCAL_ROWS
        out[row : row + LOCAL_STEPS, :] = beside
    out[TABLE_ROWS + 2 * LOCAL_ROWS :, :] = jnp.zeros(
        (GHOST_ROWS - 2 * LOCAL_ROWS, LANES), jnp.float32
    )


def first_kernel(
    tables,
    payoff,
    positions,
    offsets,
    held_tables,
    held_payoff,
    held_positions,
    held_offsets,
    plus2,
    one,
    two,
    far,
    ends,
    sem,
):
    held = (held_tables, held_payoff, held_positions, held_offsets)
    copies = [
        pltpu.make_async_copy(source, target, sem.at[i])
        for i, (source, target) in enumerate(zip((tables, payoff, positions, offsets), held))
    ]
    for copy in copies:
        copy.start()
    for copy in copies:
        copy.wait()
    pack_one(held_tables, 2, plus2, None, None)
    for side, pair, row, lane in ((0, 0, 0, 0), (1, PAIRS - LOCAL_STEPS, ROWS - 1, LANES - 1)):
        out = ends.at[side]
        for i in range(ROWS_PER_STEP):
            out[i * LOCAL_STEPS : (i + 1) * LOCAL_STEPS, :] = held_tables[
                i, pair : pair + LOCAL_STEPS, :
            ]
        out[LOCAL_ROWS : 2 * STEPS, :] = jnp.broadcast_to(
            held_payoff[row : row + 1, :], (2 * STEPS - LOCAL_ROWS, LANES)
        )
        out[2 * STEPS : HALO, :] = jnp.broadcast_to(
            held_offsets[:, lane : lane + 1].astype(jnp.float32), (STEPS, LANES)
        )
    one[...] = jnp.where(on_even_group(), ends[1], ends[0])
    two[...] = jnp.where(on_even_group(), ends[0], ends[1])
    far[...] = jnp.where(lax.axis_index("bump") == WORKERS // 2, ends[1], ends[0])


def first(*arrays):
    same = tuple(jax.ShapeDtypeStruct(array.shape, array.dtype) for array in arrays)
    message = jax.ShapeDtypeStruct((MESSAGE, LANES), jnp.float32)
    halo = jax.ShapeDtypeStruct((HALO, LANES), jnp.float32)
    return pl.pallas_call(
        first_kernel,
        out_shape=same + (message, halo, halo, halo),
        in_specs=[hbm()] * len(arrays),
        out_specs=(vmem(),) * (len(arrays) + 4),
        scratch_shapes=[
            pltpu.VMEM((2, HALO, LANES), jnp.float32),
            pltpu.SemaphoreType.DMA((len(arrays),)),
        ],
        compiler_params=params(),
        name="first",
    )(*(in_hbm(array) for array in arrays))


def pack_near_kernel(tables, one, two, own, plus1, plus3):
    before, after = halos(one, two)
    for k, out in ((1, plus1), (3, plus3), (0, own)):
        pack_one(tables, k, out, before, after)


def pack_near(tables, one, two):
    shape = jax.ShapeDtypeStruct((MESSAGE, LANES), jnp.float32)
    return pl.pallas_call(
        pack_near_kernel,
        out_shape=(shape,) * 3,
        in_specs=[vmem()] * 3,
        out_specs=(vmem(),) * 3,
        compiler_params=params(),
        name="pack",
    )(tables, one, two)


def shifted(values, by, lane):
    if by == 0:
        return values
    turned = pltpu.roll(values, (-by) % LANES, 1)
    if by > 0:
        return jnp.where(lane < LANES - by, turned, pltpu.roll(turned, PADDED - 1, 0))
    return jnp.where(lane >= -by, turned, pltpu.roll(turned, 1, 0))


def spread(low, even, down, middle, up):
    zero = jnp.zeros_like(up)
    return (
        jnp.where(low, down, zero),
        jnp.where(low, middle, jnp.where(even, down, zero)),
        jnp.where(low, up, jnp.where(even, middle, down)),
        jnp.where(low, zero, jnp.where(even, up, middle)),
        jnp.where(even, zero, up),
    )


def weigh(weights, reach):
    total = weights[0] * reach[0]
    for weight, value in zip(weights[1:], reach[1:]):
        total = total + weight * value
    return total


def roll_kernel(
    own,
    from_m1,
    from_m2,
    from_p1,
    payoff,
    positions,
    offsets,
    one,
    two,
    far,
    vol,
    out,
    sums,
    table,
    steps_k,
    nodes_k,
):
    me = lax.axis_index("bump")
    before, after = halos(one, two)
    sources = (own, from_m1, from_m2, from_p1)
    turned = jnp.transpose(offsets[...].astype(jnp.float32))
    steps_k[8 : 8 + ROWS, :] = jnp.repeat(turned, ROWS // LANES, axis=0)
    steps_k[0:8, :] = jnp.transpose(before[2 * STEPS : HALO, 0:8])
    steps_k[8 + ROWS :, :] = jnp.transpose(after[2 * STEPS : HALO, 0:8])
    start = pl.multiple_of(me * CHUNK, CHUNK)
    part = jnp.concatenate(
        [
            steps_k[pl.ds(start + 8, CHUNK + 1), :],
            jnp.zeros((PADDED - CHUNK - 2, STEPS), jnp.float32),
            steps_k[pl.ds(start + 7, 1), :],
        ]
    )
    for s in range(STEPS):
        nodes_k[s] = jnp.broadcast_to(part[:, s : s + 1], (PADDED, LANES))
    above = payoff[pl.ds(pl.multiple_of(jnp.minimum(start + CHUNK, ROWS - 8), 8), 8), :]
    below = payoff[pl.ds(pl.multiple_of(jnp.maximum(start - 8, 0), 8), 8), :]
    values = jnp.concatenate(
        [
            payoff[pl.ds(start, CHUNK), :],
            jnp.where(me == WORKERS - 1, after[LOCAL_ROWS : LOCAL_ROWS + 1, :], above[0:1, :]),
            jnp.zeros((PADDED - CHUNK - 2, LANES), jnp.float32),
            jnp.where(me == 0, before[LOCAL_ROWS : LOCAL_ROWS + 1, :], below[7:8, :]),
        ]
    )
    gap = jnp.zeros((PADDED_PAIRS - CHUNK_PAIRS - 2 * LOCAL_STEPS, LANES), jnp.float32)
    for k in range(WORKERS):
        owner = lax.bitwise_xor(me, k)
        source = sources[k]
        for i in range(ROWS_PER_STEP):
            table[owner, i, :CHUNK_PAIRS, :] = source[i * CHUNK_PAIRS : (i + 1) * CHUNK_PAIRS, :]
            at = slice(i * LOCAL_STEPS, (i + 1) * LOCAL_STEPS)
            low = TABLE_ROWS + i * LOCAL_STEPS
            high = low + LOCAL_ROWS
            ahead = source[low : low + LOCAL_STEPS, :]
            behind = source[high : high + LOCAL_STEPS, :]
            if k == 2:
                ahead = jnp.where(me == 0, far[at, :], ahead)
                behind = jnp.where(me == WORKERS - 1, far[at, :], behind)
            table[owner, i, CHUNK_PAIRS:, :] = jnp.concatenate([behind, gap, ahead])

    def rows(s, i):
        return table[s // LOCAL_STEPS, i, pl.ds(s % LOCAL_STEPS, PADDED, stride=LOCAL_STEPS), :]

    lane = lax.broadcasted_iota(jnp.int32, (PADDED, LANES), 1)
    slopes = {}
    for s in reversed(range(STEPS)):
        variance = vol[s] * vol[s]
        discount = rows(s, 0)
        up_slope = discount * rows(s, 2)
        down_slope = discount * rows(s, 4)
        up = discount * rows(s, 1) + variance * up_slope
        down = discount * rows(s, 3) + variance * down_slope
        low, even = nodes_k[s] < -0.5, nodes_k[s] < 0.5
        weights = spread(low, even, down, discount - up - down, up)
        slope_weights = spread(low, even, down_slope, -(up_slope + down_slope), up_slope)
        for q in list(slopes):
            reach = [shifted(slopes[q], m, lane) for m in range(-2, 3)]
            slopes[q] = weigh(weights, reach)
        reach = [shifted(values, m, lane) for m in range(-2, 3)]
        slopes[s] = weigh(slope_weights, reach)
        values = weigh(weights, reach)
    out[0:CHUNK, :] = values[0:CHUNK]
    weight = positions[pl.ds(start, CHUNK), :]
    lines = []
    for s in range(STEPS):
        slope = slopes[s][0:CHUNK]
        out[(s + 1) * CHUNK : (s + 2) * CHUNK, :] = slope
        lines.append(jnp.sum(weight * slope, axis=0, keepdims=True))
    totals = jnp.sum(jnp.concatenate(lines), axis=1, keepdims=True)
    step = lax.broadcasted_iota(jnp.int32, (STEPS, LANES), 0)
    own_lane = lax.broadcasted_iota(jnp.int32, (STEPS, LANES), 1) == step
    line = jnp.sum(jnp.where(own_lane, totals, 0.0), axis=0, keepdims=True)
    sums[...] = jnp.broadcast_to(line, sums.shape)


def roll_back(messages, payoff, positions, offsets, one, two, far, vol, peers):
    return pl.pallas_call(
        roll_kernel,
        out_shape=(
            jax.ShapeDtypeStruct((VALUES, LANES), jnp.float32),
            jax.ShapeDtypeStruct((peers, LANES), jnp.float32),
        ),
        in_specs=[vmem()] * (WORKERS + 6) + [smem()],
        out_specs=(vmem(), vmem()),
        scratch_shapes=[
            pltpu.VMEM((WORKERS, ROWS_PER_STEP, PADDED_PAIRS, LANES), jnp.float32),
            pltpu.VMEM((ROWS + 16, STEPS), jnp.float32),
            pltpu.VMEM((STEPS, PADDED, LANES), jnp.float32),
        ],
        compiler_params=params(),
        name="roll_back",
    )(*messages, payoff, positions, offsets, one, two, far, vol)


def build(source, tile_rows, rate, bucket, bump):
    base = source[0:CHUNK, :]
    for b in range(CURVES):
        gain = bump[b] * rate[b]
        slope = source[pl.ds(pl.multiple_of((bucket[b] + 1) * CHUNK, CHUNK), CHUNK), :]
        tile_rows[b // 8, pl.ds(b % 8, CHUNK, stride=8), :] = base + gain * slope


def write(built, out, chunk, sems):
    stores = []
    for tile in range(CURVES // 8):
        rows = pl.ds(pl.multiple_of(chunk * CHUNK * 8, CHUNK * 8), CHUNK * 8)
        stores.append(pltpu.make_async_copy(built.at[tile], out.at[tile, rows, :], sems.at[tile]))
        stores[-1].start()
    return stores


def rates(vol, bucket, bump):
    return [2.0 * vol[bucket[b]] + bump[b] for b in range(CURVES)]


def expand_chunks(parts, vol, bucket, bump, out, built, done):
    me = lax.axis_index("bump")
    rate = rates(vol, bucket, bump)
    stores = []
    for k, (source, flip) in enumerate(parts):
        build(source, built.at[k], rate, bucket, bump)
        stores += write(built.at[k], out, lax.bitwise_xor(me, flip), done.at[k])
    for store in stores:
        store.wait()


def expand_kernel(own, from_1, from_3, vol, bucket, bump, out, built, done):
    parts = ((own, 0), (from_1, 1), (from_3, 3))
    expand_chunks(parts, vol, bucket, bump, out, built, done)


def scratch(chunks):
    tiles = CURVES // 8
    return [
        pltpu.VMEM((chunks, tiles, CHUNK * 8, LANES), jnp.float32),
        pltpu.SemaphoreType.DMA((chunks, tiles)),
    ]


def expand(own, from_1, from_3, vol, bucket, bump):
    return pl.pallas_call(
        expand_kernel,
        out_shape=jax.ShapeDtypeStruct((CURVES // 8, ROWS * 8, LANES), jnp.float32),
        in_specs=[vmem()] * 3 + [smem()] * 3,
        out_specs=anywhere(),
        scratch_shapes=scratch(3),
        compiler_params=params(),
        cost_estimate=EXPAND_COST,
        name="expand",
    )(own, from_1, from_3, vol, bucket, bump)


def complete_kernel(low, high, vol, bucket, bump, started, out, picks, joined, built, done):
    del started
    rate = rates(vol, bucket, bump)
    row = lax.broadcasted_iota(jnp.int32, (CURVES, LANES), 0)
    lane = lax.broadcasted_iota(jnp.int32, (CURVES, LANES), 1)
    pick = jnp.zeros((CURVES, LANES), jnp.float32)
    for b in range(CURVES):
        pick = jnp.where(jnp.logical_and(row == b, lane == bucket[b]), rate[b], pick)
    picks[...] = pick
    joined[0:HALF, :] = low[...]
    joined[HALF:, :] = high[...]
    expand_chunks(((joined, 2),), vol, bucket, bump, out, built, done)


def complete(low, high, vol, bucket, bump, started):
    tiles = CURVES // 8
    laid, picks = pl.pallas_call(
        complete_kernel,
        out_shape=(
            jax.ShapeDtypeStruct(started.shape, started.dtype),
            jax.ShapeDtypeStruct((CURVES, LANES), jnp.float32),
        ),
        in_specs=[vmem()] * 2 + [smem()] * 3 + [anywhere()],
        out_specs=(anywhere(), vmem()),
        scratch_shapes=[pltpu.VMEM((VALUES, LANES), jnp.float32)] + scratch(1),
        input_output_aliases={5: 0},
        compiler_params=params(),
        cost_estimate=EXPAND_COST,
        name="complete",
    )(low, high, vol, bucket, bump, started)
    curves = laid.reshape(tiles, ROWS, 8, LANES).transpose(0, 2, 1, 3)
    return curves.reshape(CURVES, ROWS * LANES), picks


def vega_kernel(shared, picks, vega):
    totals = jnp.sum(shared[...], axis=0, keepdims=True)
    entry = jnp.sum(picks[...] * totals, axis=1, keepdims=True)
    row = lax.broadcasted_iota(jnp.int32, (CURVES, LANES), 0)
    lane = lax.broadcasted_iota(jnp.int32, (CURVES, LANES), 1)
    line = jnp.sum(jnp.where(lane == row, entry, 0.0), axis=0, keepdims=True)
    vega[...] = line[:, :CURVES]


def vegas(shared, picks):
    return pl.pallas_call(
        vega_kernel,
        out_shape=jax.ShapeDtypeStruct((1, CURVES), jnp.float32),
        in_specs=[vmem(), vmem()],
        out_specs=vmem(),
        compiler_params=params(),
        name="vegas",
    )(shared, picks).reshape(CURVES)


def rotated(by):
    return [(i, (i + by) % WORKERS) for i in range(WORKERS)]


def on_device(payoff, positions, tables, offsets, vol_curve, bucket, bump_size):
    groups = lax.axis_size(NODE_AXES)
    with_next = [(i, i ^ 1) for i in range(groups)]
    with_last = [(i, (i + (1 if i % 2 else groups - 1)) % groups) for i in range(groups)]
    payoff_rows = payoff.reshape(ROWS, LANES)
    tables = tables.transpose(1, 0, 2).reshape(ROWS_PER_STEP, LOCAL_STEPS, ROWS, LANES)
    tables = tables.transpose(0, 2, 1, 3).reshape(ROWS_PER_STEP, PAIRS, LANES)
    to_ends = [(2 * groups + i, (i + 1) % groups) for i in range(groups)]
    to_ends += [(groups + i, 3 * groups + (i + groups - 1) % groups) for i in range(groups)]
    held, payoff_rows, position_rows, offsets, plus2, one, two, far = first(
        tables, payoff_rows, positions.reshape(ROWS, LANES), offsets
    )
    far = lax.ppermute(far, ALL_AXES, to_ends)
    from_m2 = lax.ppermute(plus2, "bump", rotated(2))
    one = lax.ppermute(one, NODE_AXES, with_next)
    two = lax.ppermute(two, NODE_AXES, with_last)
    own, plus1, plus3 = pack_near(held, one, two)
    received = (
        own,
        lax.ppermute(plus1, "bump", [(i, i ^ 1) for i in range(WORKERS)]),
        from_m2,
        lax.ppermute(plus3, "bump", [(i, i ^ 3) for i in range(WORKERS)]),
    )
    peers = lax.axis_size(ALL_AXES)
    arrays, sums = roll_back(
        received, payoff_rows, position_rows, offsets, one, two, far, vol_curve, peers
    )
    pairs = {flip: [(i, i ^ flip) for i in range(WORKERS)] for flip in (1, 3)}
    from_1 = lax.ppermute(arrays, "bump", pairs[1])
    from_3 = lax.ppermute(arrays, "bump", pairs[3])
    low = lax.ppermute(from_3[:HALF], "bump", pairs[1])
    high = lax.ppermute(from_1[HALF:], "bump", pairs[3])
    started = expand(arrays, from_1, from_3, vol_curve, bucket, bump_size)
    bumped_values, picks = complete(low, high, vol_curve, bucket, bump_size, started)
    shared = lax.all_to_all(
        sums.reshape(peers, 1, LANES), ALL_AXES, split_axis=0, concat_axis=0, tiled=True
    )
    return (bumped_values, vegas(shared.reshape(peers, LANES), picks))


def solution(mesh):
    in_specs = (
        P(("nx", "ny")),
        P(("nx", "ny")),
        P("bump", None, ("nx", "ny")),
        P(None, ("nx", "ny")),
        P(),
        P("bump"),
        P("bump"),
    )
    out_specs = (P("bump", ("nx", "ny")), P("bump"))
    return jax.shard_map(
        on_device, mesh=mesh, in_specs=in_specs, out_specs=out_specs, check_vma=False
    )
```
